256 devices in a mesh: segment: 8 (over x_hi, y), tp: 32 (over x_lo, z, core).
Axes of the slice: x: 4 (x_hi: 2, x_lo: 2; x = x_hi * 2 + x_lo), y: 4, z: 8, core: 2. Of those that a mesh axis runs over, the one named last changes fastest.
Arguments:
- queries: bfloat16 [256, 256, 8192], P(('segment', 'tp'))
- caption_kv: bfloat16 [256, 256, 2048], P(('segment', 'tp')), may hold values from -6 to 6
- caption_len: int32 [256], P(('segment', 'tp')), may hold values from 64 to 256
- image_kv: bfloat16 [256, 48, 2048], P(('segment', 'tp')), may hold values from -6 to 6
- patch_count: int32 [256], replicated, may hold values from 12 to 48
- image_list: int32 [32, 8], replicated, may hold values from 0 to 255, as said below
- pref_order: int32 [32, 8], replicated, may hold values from 0 to 7, each once within a row
- reward_dir: float32 [8192], replicated, may hold values from -1.8 to 1.8
Outputs:
- loss_total: float32 [], replicated
- rewards: float32 [256], P(('segment', 'tp'))
- image_grad: float32 [256, 48, 2048], P(('segment', 'tp'))
The draws below stay inside these ranges and needn't reach their ends.
Inputs may be any that keep to these rules, and one draw needn't show every extreme that they name: `image_list`: the image in place j of a group g has its id in the block of device (section s, column (g % 4) * 8 + j) for some section s: ids run by owner, section-major, 1 per owner, so device (s, c) owns ids (s * 32 + c) * 1 onward. Group g lies in section g // 4. `pref_order`: each row is a ranking of the 8 captions of its group.
All inputs are finite; a program needn't handle non-finite values.
Results may differ from the reference program's by a relative error of at most 0.03.
Values may be sent and summed in bfloat16 or wider, within the bound.
No kernel may reach another device: no remote copies, remote signals or barrier semaphores. Data moves between devices by JAX's collectives and lax.ppermute only.
A program may use at most 128 MiB of HBM per device.

```python
import math
import jax
import jax.numpy as jnp
from jax import lax

D = 8192
KV_HEADS = 8
HEAD_DIM = 128
CAP_LEN = 256
PATCHES = 48
IMG_DEV = 1
CAPS = 8
GROUP_HEADS = 8
KV_WIDTH = 2048
CAPTIONS = 256
GROUPS = 32
GRP_ST = 4
COLUMNS = 32
SECTIONS = 8
NIMG = 256


def draw_queries(key, part):
    key = jax.random.fold_in(key, 11)
    normal_key = jax.random.fold_in(key, 0)
    normal_base = jnp.clip(jax.random.normal(normal_key, (CAPTIONS, CAP_LEN, D), jnp.float32), -6.0, 6.0)
    return normal_base.astype(jnp.bfloat16)


def draw_image_list(key, part):
    key = jax.random.fold_in(key, 23)
    section_key, remainder_key = jax.random.split(key)
    group_ids = jnp.arange(GROUPS, dtype=jnp.int32)[:, None]
    places = jnp.arange(CAPS, dtype=jnp.int32)[None, :]
    column = group_ids % GRP_ST * CAPS + places
    section = jax.random.randint(section_key, (GROUPS, CAPS), 0, SECTIONS, dtype=jnp.int32)
    remainder = jax.random.randint(remainder_key, (GROUPS, CAPS), 0, IMG_DEV, dtype=jnp.int32)
    return ((section * COLUMNS + column) * IMG_DEV + remainder).astype(jnp.int32)


def touch_ends(result, rng, smallest, top_value):
    extent = result.shape
    index_at = [jax.random.randint(jax.random.fold_in(rng, axis), (), 0, extent[axis]) for axis in range(len(extent))]
    result = result.at[tuple(index_at)].set(smallest)
    longest = extent.index(max(extent))
    index_at[longest] = (index_at[longest] + 1) % extent[longest]
    return result.at[tuple(index_at)].set(top_value)


def levels(rng, shape, cuts, smallest, high):
    def one(dim, shards_of):
        draws = jax.random.uniform(jax.random.fold_in(jax.random.fold_in(rng, 6), dim), (shards_of,), jnp.float32, smallest / len(cuts), high / len(cuts))
        return jnp.repeat(jnp.exp(draws), shape[dim] // shards_of).reshape((-1,) + (1,) * (len(shape) - dim - 1))

    gain = one(*cuts[0])
    for cut in cuts[1:]:
        gain = gain * one(*cut)
    return gain


def normal_values(rng, dims, deviation, reach, cuts=(), kind=jnp.bfloat16):
    factor_of = levels(rng, dims, cuts, -0.22, 0.18) if cuts else 1.0
    drawn = jax.random.normal(rng, dims, jnp.float32) * deviation * factor_of
    return jnp.minimum(jnp.maximum(drawn, -reach), reach).astype(kind)


def setup_inputs(seed: int = 0) -> dict:
    splits = jax.random.split(jax.random.key(seed), 9)
    queries = draw_queries(jax.random.fold_in(splits[8], 71), 0)
    caption_kv = normal_values(splits[1], (CAPTIONS, CAP_LEN, KV_WIDTH), 1.0, 6.0, ((0, 256),))
    caption_len = touch_ends(jax.random.randint(splits[2], (CAPTIONS,), CAP_LEN // 4, CAP_LEN + 1), jax.random.fold_in(splits[2], 1), CAP_LEN // 4, CAP_LEN).astype(jnp.int32)
    image_kv = normal_values(splits[3], (NIMG, PATCHES, KV_WIDTH), 1.0, 6.0, ((0, 256),))
    patch_count = touch_ends(jax.random.randint(splits[4], (NIMG,), PATCHES // 4, PATCHES + 1), jax.random.fold_in(splits[4], 1), PATCHES // 4, PATCHES).astype(jnp.int32)
    image_list = draw_image_list(jax.random.fold_in(splits[8], 71), 0)
    pref_order = jax.vmap(lambda own: jax.random.permutation(own, CAPS))(jax.random.split(splits[6], GROUPS)).reshape((GROUPS, CAPS)).astype(jnp.int32)
    reward_dir = normal_values(splits[7], (D,), 0.3, 1.8, (), jnp.float32)
    return dict(queries=queries, caption_kv=caption_kv, caption_len=caption_len, image_kv=image_kv, patch_count=patch_count, image_list=image_list, pref_order=pref_order, reward_dir=reward_dir)


norm_eps = 1e-06
loss_scale = 65536.0

def head_scores(query_head, key_head, key_valid, scaling):
    scores = jnp.einsum('tgd,kd->gtk', query_head.astype(jnp.float32), key_head.astype(jnp.float32)) * scaling
    return jnp.where(key_valid[None], scores, -jnp.inf)

def head_forward(members, key_valid, scaling):
    query_head, key_head, value_head = members
    scores = head_scores(query_head, key_head, key_valid, scaling)
    row_max = lax.optimization_barrier(jnp.max(scores, axis=-1, keepdims=True))
    exponent = jnp.exp(scores - row_max)
    totals = lax.optimization_barrier(jnp.sum(exponent, axis=-1, keepdims=True))
    weights = (exponent / totals).astype(jnp.bfloat16)
    output = jnp.einsum('gtk,kd->tgd', weights.astype(jnp.float32), value_head.astype(jnp.float32))
    return (output, row_max, totals)

def caption_forward(query_rows, own_kv, group_images, counts, length, direction):
    scaling = 1.0 / math.sqrt(HEAD_DIM)
    query_heads = query_rows.reshape(CAP_LEN, KV_HEADS, GROUP_HEADS, HEAD_DIM).transpose(1, 0, 2, 3)
    image_tokens = group_images.reshape(CAPS * PATCHES, 2, KV_HEADS, HEAD_DIM)
    own_tokens = own_kv.reshape(CAP_LEN, 2, KV_HEADS, HEAD_DIM)
    keys_all = jnp.concatenate([image_tokens[:, 0], own_tokens[:, 0]], axis=0).transpose(1, 0, 2)
    values_all = jnp.concatenate([image_tokens[:, 1], own_tokens[:, 1]], axis=0).transpose(1, 0, 2)
    image_valid = (jnp.arange(PATCHES, dtype=jnp.int32)[None, :] < counts[:, None]).reshape(-1)
    token_pos = jnp.arange(CAP_LEN, dtype=jnp.int32)
    own_valid = token_pos[None, :] <= token_pos[:, None]
    key_valid = jnp.concatenate([jnp.broadcast_to(image_valid[None, :], (CAP_LEN, CAPS * PATCHES)), own_valid], axis=1)
    outputs, maxima, totals = lax.map(lambda members: head_forward(members, key_valid, scaling), (query_heads, keys_all, values_all))
    attended = outputs.transpose(1, 0, 2, 3).reshape(CAP_LEN, D)
    inv_rms = lax.rsqrt(lax.optimization_barrier(jnp.mean(attended * attended, axis=-1, keepdims=True)) + norm_eps)
    normed = attended * inv_rms
    per_token = lax.optimization_barrier(jnp.sum(normed * direction[None, :], axis=-1))
    live_rows = token_pos < length
    length_f = length.astype(jnp.float32)
    reward = jnp.sum(jnp.where(live_rows, per_token, 0.0)) / length_f
    cached = (query_heads, keys_all, values_all, key_valid, attended, normed, inv_rms, maxima, totals, live_rows)
    return (reward, cached)

def head_backward(members, key_valid, scaling):
    query_head, key_head, value_head, grad_head, row_max, totals, delta_head = members
    scores = head_scores(query_head, key_head, key_valid, scaling)
    probs = jnp.exp(scores - row_max) / totals
    weights = probs.astype(jnp.bfloat16)
    value_grad = jnp.einsum('gtk,tgd->kd', weights.astype(jnp.float32), grad_head.astype(jnp.float32))
    weight_grad = jnp.einsum('tgd,kd->gtk', grad_head.astype(jnp.float32), value_head.astype(jnp.float32))
    score_grad = (probs * (weight_grad - delta_head[..., None])).astype(jnp.bfloat16)
    key_grad = jnp.einsum('gtk,tgd->kd', score_grad.astype(jnp.float32), query_head.astype(jnp.float32)) * scaling
    return (key_grad, value_grad)

def caption_backward(cached, length, direction, scaled_grad):
    scaling = 1.0 / math.sqrt(HEAD_DIM)
    query_heads, keys_all, values_all, key_valid, attended, normed, inv_rms, maxima, totals, live_rows = cached
    image_keys = CAPS * PATCHES
    length_f = length.astype(jnp.float32)
    normed_grad = jnp.where(live_rows[:, None], direction[None, :] * (scaled_grad / length_f), 0.0)
    att_grad = inv_rms * (normed_grad - normed * lax.optimization_barrier(jnp.mean(normed_grad * normed, axis=-1, keepdims=True)))
    att_grad_b = att_grad.astype(jnp.bfloat16)
    grad_heads = att_grad_b.reshape(CAP_LEN, KV_HEADS, GROUP_HEADS, HEAD_DIM).transpose(1, 0, 2, 3)
    delta_rows = lax.optimization_barrier(jnp.sum((att_grad_b.astype(jnp.float32) * attended).reshape(CAP_LEN, KV_HEADS, GROUP_HEADS, HEAD_DIM), axis=-1)).transpose(1, 2, 0)
    image_valid = key_valid[:, :image_keys]
    key_grads, value_grads = lax.map(lambda members: head_backward(members, image_valid, scaling), (query_heads, keys_all[:, :image_keys], values_all[:, :image_keys], grad_heads, maxima, totals, delta_rows))
    stacked = jnp.stack([key_grads, value_grads], axis=0).transpose(2, 0, 1, 3)
    return stacked.reshape(CAPS, PATCHES, KV_WIDTH)

def group_loss(group_rewards, ranking):
    ranked = jnp.take(group_rewards, ranking)
    rank_pos = jnp.arange(CAPS, dtype=jnp.int32)
    upper_pairs = rank_pos[:, None] < rank_pos[None, :]
    margins = ranked[None, :] - ranked[:, None]
    return jnp.sum(jnp.where(upper_pairs, jax.nn.softplus(margins), 0.0))

def reference(queries, caption_kv, caption_len, image_kv, patch_count, image_list, pref_order, reward_dir):

    def forward_one(caption_idx):
        image_ids = image_list[caption_idx // CAPS]
        group_images = jnp.take(image_kv, image_ids, axis=0)
        counts = jnp.take(patch_count, image_ids)
        reward, cached = caption_forward(queries[caption_idx], caption_kv[caption_idx], group_images, counts, caption_len[caption_idx], reward_dir)
        return reward
    indices = jnp.arange(CAPTIONS, dtype=jnp.int32)
    rewards = lax.map(forward_one, indices)
    grouped = rewards.reshape(GROUPS, CAPS)
    loss_total = jnp.sum(jax.vmap(group_loss)(grouped, pref_order))
    reward_grads = jax.vmap(jax.grad(group_loss))(grouped, pref_order).reshape(-1)

    def back_step(accumulated, caption_idx):
        image_ids = image_list[caption_idx // CAPS]
        group_images = jnp.take(image_kv, image_ids, axis=0)
        counts = jnp.take(patch_count, image_ids)
        reward, cached = caption_forward(queries[caption_idx], caption_kv[caption_idx], group_images, counts, caption_len[caption_idx], reward_dir)
        grads = caption_backward(cached, caption_len[caption_idx], reward_dir, loss_scale * reward_grads[caption_idx])
        return (accumulated.at[image_ids].add(grads), None)
    image_grad, unused = lax.scan(back_step, jnp.zeros((NIMG, PATCHES, KV_WIDTH), jnp.float32), indices)
    return (loss_total, rewards, image_grad)
```

```python
import math

import jax
import jax.numpy as jnp
from jax import lax
from jax.experimental import pallas as pl
from jax.experimental.pallas import tpu as pltpu
from jax.sharding import PartitionSpec as P

D = 8192
KV_HEADS = 8
HEAD_DIM = 128
CAP_LEN = 256
PATCHES = 48
CAPS = 8
GROUP_HEADS = 8
KV_WIDTH = 2048
COLUMNS = 32
IMG_SLOTS = CAPS * PATCHES
COEFS = KV_HEADS * GROUP_HEADS
WIDE = KV_WIDTH + 2 * COEFS
HALF = CAP_LEN // 2

norm_eps = 1e-06
loss_scale = 65536.0
scaling = 1.0 / math.sqrt(HEAD_DIM)
to_base2 = scaling * math.log2(math.e)

SMEM = pltpu.SMEM
VMEM = pltpu.VMEM
VMEM_LIMIT = 24 * 1024 * 1024

AT_Y, AT_SRC_Y, AT_SRC_X_SAME, AT_PARTNER_Y, AT_PLACE, AT_LEN = 0, 1, 2, 3, 4, 5
AT_COUNTS, AT_RANKING, AT_DEST = 8, 16, 24

REL = (0, 2, 4, 6, 1, 3, 5, 7)

SUM_LOW, SUM_HIGH = 2.0**-40, 2.0**60


def exact_dot(a, b, dims):
    return lax.dot_general(a, b, (dims, ((), ())), preferred_element_type=jnp.float32)


def meta_kernel(idx_ref, list_ref, count_ref, order_ref, len_ref, out_ref):
    seg = idx_ref[0]
    col = idx_ref[1]
    x = seg // 4
    y = seg % 4
    slot = col // CAPS
    place = col % CAPS

    def section_of(section):
        return list_ref[section * 4 + slot, place] // COLUMNS

    own = section_of(seg)
    partner = section_of((1 - x) * 4 + y)
    out_ref[AT_Y] = y
    out_ref[AT_SRC_Y] = own % 4
    out_ref[AT_SRC_X_SAME] = (own // 4 == x).astype(jnp.int32)
    out_ref[AT_PARTNER_Y] = partner % 4
    out_ref[AT_PLACE] = place
    out_ref[AT_LEN] = len_ref[0]
    group = seg * 4 + slot
    for i, rel in enumerate(REL):
        out_ref[AT_COUNTS + i] = count_ref[list_ref[group, place ^ rel]]
    for k in range(CAPS):
        out_ref[AT_RANKING + k] = order_ref[group, k]
    for k in range(4):
        dest = section_of(x * 4 + (y + 4 - k) % 4)
        here = (dest % 4 == y).astype(jnp.int32)
        out_ref[AT_DEST + k] = here * jnp.where(dest // 4 == x, 1, 2)


def make_meta(idx, image_list, patch_count, pref_order, caption_len):
    smem = pl.BlockSpec(memory_space=SMEM)
    return pl.pallas_call(
        meta_kernel,
        out_shape=jax.ShapeDtypeStruct((32,), jnp.int32),
        in_specs=[smem] * 5,
        out_specs=smem,
        name="meta",
    )(idx, image_list, patch_count, pref_order, caption_len)


def pick_partner_kernel(meta_ref, i0, i1, i2, i3, out_ref, sem):
    y = meta_ref[AT_Y]
    back = (y + 4 - meta_ref[AT_PARTNER_Y]) % 4
    for k, src in enumerate((i0, i1, i2, i3)):

        @pl.when(back == k)
        def _():
            copy = pltpu.make_async_copy(src, out_ref, sem)
            copy.start()
            copy.wait()


def pick_own_kernel(meta_ref, i0, i1, i2, i3, far, out_ref, sem):
    y = meta_ref[AT_Y]
    same = meta_ref[AT_SRC_X_SAME]
    back = jnp.where(same == 1, (y + 4 - meta_ref[AT_SRC_Y]) % 4, 4)
    for k, src in enumerate((i0, i1, i2, i3, far)):

        @pl.when(back == k)
        def _():
            copy = pltpu.make_async_copy(src, out_ref, sem)
            copy.start()
            copy.wait()


def pick(kernel, name, meta, *images):
    any_space = pl.BlockSpec(memory_space=pl.ANY)
    return pl.pallas_call(
        kernel,
        out_shape=jax.ShapeDtypeStruct(images[0].shape, images[0].dtype),
        in_specs=[pl.BlockSpec(memory_space=SMEM)] + [any_space] * len(images),
        out_specs=pl.BlockSpec(memory_space=VMEM),
        scratch_shapes=[pltpu.SemaphoreType.DMA],
        name=name,
    )(meta, *images)


def forward_kernel(meta_ref, q_ref, own_k_ref, own_v_ref, dir_ref, *rest):
    images = rest[:CAPS]
    p_ref, att_ref, inv_ref, stat_ref, reward_ref, ss_ref, rd_ref = rest[CAPS:]
    head = pl.program_id(0)
    key_cols = pl.ds(pl.multiple_of(head * HEAD_DIM, HEAD_DIM), HEAD_DIM)
    value_cols = pl.ds(pl.multiple_of((KV_HEADS + head) * HEAD_DIM, HEAD_DIM), HEAD_DIM)

    row = lax.broadcasted_iota(jnp.int32, (PATCHES, HEAD_DIM), 0)
    keys, values, marks = [], [], []
    for i, image in enumerate(images):
        live = row < meta_ref[AT_COUNTS + i]
        key = image[:, key_cols].astype(jnp.float32)
        keys.append(jnp.where(live, key, key[0:1, :]).astype(jnp.bfloat16))
        values.append(jnp.where(live, image[:, value_cols].astype(jnp.float32), 0.0))
        marks.append(live.astype(jnp.float32))
    image_keys = jnp.concatenate(keys, axis=0)
    own_keys = own_k_ref[...]
    values.append(own_v_ref[...].astype(jnp.float32))
    marks.append(jnp.ones((CAP_LEN, HEAD_DIM), jnp.float32))
    values_t = jnp.concatenate(values, axis=0).T
    marks_t = jnp.concatenate(marks, axis=0).T[:16]
    mixed = jnp.concatenate([values_t, marks_t], axis=0).astype(jnp.bfloat16)
    dir_t = dir_ref[...].T

    @pl.when(head == 0)
    def _():
        ss_ref[...] = jnp.zeros_like(ss_ref)
        rd_ref[...] = jnp.zeros_like(rd_ref)

    diagonal = lax.broadcasted_iota(jnp.int32, (HALF, HALF), 0) <= lax.broadcasted_iota(
        jnp.int32, (HALF, HALF), 1
    )
    minus = jnp.full((HALF, HALF), -jnp.inf, jnp.float32)

    def query(g):
        return q_ref[:, pl.ds(g * HEAD_DIM, HEAD_DIM)]

    def scores(g):
        q = query(g)
        s_img = exact_dot(image_keys, q, ((1,), (1,)))
        s_own = exact_dot(own_keys, q, ((1,), (1,)))
        return s_img, s_own

    def finish(g, p_all):
        out = exact_dot(mixed, p_all, ((1,), (0,)))
        total = out[HEAD_DIM : HEAD_DIM + 8]
        inv = 1.0 / total
        att = (out[:HEAD_DIM].reshape(16, 8, CAP_LEN) * inv[None]).reshape(HEAD_DIM, CAP_LEN)
        att_ref[pl.ds(g * HEAD_DIM, HEAD_DIM), :] = att
        inv_ref[pl.ds(g, 1), :] = inv[:1]
        return total

    def square_and_reward(g, dir_col):
        att = att_ref[pl.ds(g * HEAD_DIM, HEAD_DIM), :]
        ss = jnp.sum((att * att).reshape(16, 8, CAP_LEN), axis=0)
        rd = jnp.sum((att * dir_col).reshape(16, 8, CAP_LEN), axis=0)
        return ss, rd

    def own_block(p_a, p_b, p_c):
        return jnp.concatenate(
            [
                jnp.concatenate([p_a, p_b], axis=1),
                jnp.concatenate([jnp.zeros_like(p_c), p_c], axis=1),
            ],
            axis=0,
        )

    def plain(s, keep=None):
        s = s * to_base2
        if keep is not None:
            s = jnp.where(keep, s, minus)
        return jnp.exp2(s).astype(jnp.bfloat16)

    low = jnp.full((8, CAP_LEN), jnp.inf, jnp.float32)
    high = jnp.zeros((8, CAP_LEN), jnp.float32)
    ahead = scores(0)
    before = None
    for g in range(GROUP_HEADS + 1):
        if g < GROUP_HEADS:
            s_img, s_own = ahead
            if g + 1 < GROUP_HEADS:
                ahead = scores(g + 1)
            p_img = plain(s_img)
            p_ref[g] = p_img
            p_own = own_block(
                plain(s_own[:HALF, :HALF], diagonal),
                plain(s_own[:HALF, HALF:]),
                plain(s_own[HALF:, HALF:], diagonal),
            )
            p_all = jnp.concatenate([p_img, p_own], axis=0)
        if g > 0:
            total = finish(g - 1, before)
            low = jnp.minimum(low, total)
            high = jnp.maximum(high, total)
        before = p_all
    inside = jnp.all((low > SUM_LOW) & (high < SUM_HIGH))

    @pl.when(jnp.logical_not(inside))
    def _():
        @pl.loop(0, GROUP_HEADS)
        def _(g):
            s_img, s_own = scores(g)
            s_a = jnp.where(diagonal, s_own[:HALF, :HALF], minus)
            s_b = s_own[:HALF, HALF:]
            s_c = jnp.where(diagonal, s_own[HALF:, HALF:], minus)
            m_low = jnp.max(s_a, axis=0, keepdims=True)
            m_high = jnp.max(jnp.maximum(s_b, s_c), axis=0, keepdims=True)
            m = jnp.maximum(
                jnp.max(s_img, axis=0, keepdims=True), jnp.concatenate([m_low, m_high], axis=1)
            )
            m_low, m_high = m[:, :HALF], m[:, HALF:]
            p_img = jnp.exp2((s_img - m) * to_base2).astype(jnp.bfloat16)
            p_ref[g] = p_img
            p_own = own_block(
                jnp.exp2((s_a - m_low) * to_base2).astype(jnp.bfloat16),
                jnp.exp2((s_b - m_high) * to_base2).astype(jnp.bfloat16),
                jnp.exp2((s_c - m_high) * to_base2).astype(jnp.bfloat16),
            )
            finish(g, jnp.concatenate([p_img, p_own], axis=0))

    ss = ss_ref[...]
    rd = rd_ref[...]
    for g in range(GROUP_HEADS):
        ss_g, rd_g = square_and_reward(g, dir_t[:, g : g + 1])
        ss = ss + ss_g
        rd = rd + rd_g
    ss_ref[...] = ss
    rd_ref[...] = rd

    @pl.when(head == KV_HEADS - 1)
    def _():
        length = meta_ref[AT_LEN]
        inv_rms = lax.rsqrt(jnp.sum(ss, axis=0, keepdims=True) * (1.0 / D) + norm_eps)
        per_token = jnp.sum(rd, axis=0, keepdims=True) * inv_rms
        live = lax.broadcasted_iota(jnp.int32, (1, CAP_LEN), 1) < length
        length_f = jnp.full((1, CAP_LEN), length, jnp.int32).astype(jnp.float32)
        unit = jnp.where(live, 1.0 / length_f, 0.0)
        a = inv_rms * unit
        b = inv_rms * inv_rms * unit * per_token * (1.0 / D)
        stat_ref[...] = jnp.concatenate([a, b, jnp.zeros((6, CAP_LEN), jnp.float32)], axis=0)
        reward = jnp.sum(jnp.where(live, per_token, 0.0), axis=1, keepdims=True)
        reward_ref[...] = jnp.broadcast_to(reward / length_f[:, :1], (8, 128))


def forward(meta, q, own_kv, direction, images):
    whole = pl.BlockSpec((PATCHES, KV_WIDTH), lambda h: (0, 0))
    rows = GROUP_HEADS * HEAD_DIM
    return pl.pallas_call(
        forward_kernel,
        grid=(KV_HEADS,),
        in_specs=[
            pl.BlockSpec(memory_space=SMEM),
            pl.BlockSpec((CAP_LEN, rows), lambda h: (0, h)),
            pl.BlockSpec((CAP_LEN, HEAD_DIM), lambda h: (0, h)),
            pl.BlockSpec((CAP_LEN, HEAD_DIM), lambda h: (0, KV_HEADS + h)),
            pl.BlockSpec((GROUP_HEADS, HEAD_DIM), lambda h: (h, 0)),
        ]
        + [whole] * CAPS,
        out_specs=[
            pl.BlockSpec((GROUP_HEADS, IMG_SLOTS, CAP_LEN), lambda h: (h, 0, 0)),
            pl.BlockSpec((rows, CAP_LEN), lambda h: (h, 0)),
            pl.BlockSpec((GROUP_HEADS, CAP_LEN), lambda h: (h, 0)),
            pl.BlockSpec((8, CAP_LEN), lambda h: (0, 0)),
            pl.BlockSpec((8, 128), lambda h: (0, 0)),
        ],
        out_shape=[
            jax.ShapeDtypeStruct((KV_HEADS * GROUP_HEADS, IMG_SLOTS, CAP_LEN), jnp.bfloat16),
            jax.ShapeDtypeStruct((D, CAP_LEN), jnp.float32),
            jax.ShapeDtypeStruct((KV_HEADS * GROUP_HEADS, CAP_LEN), jnp.float32),
            jax.ShapeDtypeStruct((8, CAP_LEN), jnp.float32),
            jax.ShapeDtypeStruct((8, 128), jnp.float32),
        ],
        scratch_shapes=[VMEM((8, CAP_LEN), jnp.float32), VMEM((8, CAP_LEN), jnp.float32)],
        compiler_params=pltpu.CompilerParams(vmem_limit_bytes=VMEM_LIMIT),
        cost_estimate=pl.CostEstimate(
            flops=5_400_000_000, bytes_accessed=28_000_000, transcendentals=10_000_000
        ),
        name="forward",
    )(meta, q, own_kv, own_kv, direction, *images)


def backward_kernel(meta_ref, stat_ref, q_ref, dir_ref, p_ref, att_ref, inv_ref, *rest):
    images = rest[:CAPS]
    keep_ref, send_ref, coef_ref = rest[CAPS:]
    head = pl.program_id(0)
    key_cols = pl.ds(pl.multiple_of(head * HEAD_DIM, HEAD_DIM), HEAD_DIM)
    value_cols = pl.ds(pl.multiple_of((KV_HEADS + head) * HEAD_DIM, HEAD_DIM), HEAD_DIM)
    values = jnp.concatenate([image[:, value_cols] for image in images], axis=0)
    dir_t = dir_ref[...].T
    a = stat_ref[0:1, :]
    b = stat_ref[1:2, :]
    key_grad = jnp.zeros((IMG_SLOTS, HEAD_DIM), jnp.float32)
    value_grad = jnp.zeros((IMG_SLOTS, 2 * HEAD_DIM), jnp.float32)
    which = lax.broadcasted_iota(jnp.int32, (HEAD_DIM, CAP_LEN), 0)

    @pl.when(head == 0)
    def _():
        coef_ref[...] = jnp.zeros_like(coef_ref)

    for g in range(GROUP_HEADS):
        q = q_ref[:, g * HEAD_DIM : (g + 1) * HEAD_DIM]
        att = att_ref[g * HEAD_DIM : (g + 1) * HEAD_DIM, :]
        inv = inv_ref[g : g + 1, :]
        factor = a * inv
        rest_grad = -(b * inv) * att
        grad = (factor * dir_t[:, g : g + 1] + rest_grad).astype(jnp.bfloat16)
        delta = jnp.sum(grad.astype(jnp.float32) * att, axis=0, keepdims=True)
        factors = jnp.where(which == head * GROUP_HEADS + g, factor, 0.0)
        apart = jnp.concatenate([rest_grad, factors], axis=0).astype(jnp.bfloat16)
        p = p_ref[g]
        value_grad = value_grad + exact_dot(p, apart, ((1,), (1,)))
        weight_grad = exact_dot(values, grad, ((1,), (0,)))
        score_grad = (p.astype(jnp.float32) * (weight_grad - delta)).astype(jnp.bfloat16)
        key_grad = key_grad + exact_dot(score_grad, q, ((1,), (0,)))
    key_grad = key_grad * scaling
    row = lax.broadcasted_iota(jnp.int32, (PATCHES, HEAD_DIM), 0)
    for i in range(CAPS):
        live = row < meta_ref[AT_COUNTS + i]
        out_ref = keep_ref if i < 4 else send_ref
        part = slice(i * PATCHES, (i + 1) * PATCHES)
        out_ref[i % 4, :, key_cols] = jnp.where(live, key_grad[part], 0.0).astype(jnp.bfloat16)
        out_ref[i % 4, :, value_cols] = jnp.where(live, value_grad[part, :HEAD_DIM], 0.0).astype(jnp.bfloat16)
    coef_ref[...] += value_grad[:, HEAD_DIM:]

    @pl.when(head == KV_HEADS - 1)
    def _():
        for i in range(CAPS):
            live = row < meta_ref[AT_COUNTS + i]
            out_ref = keep_ref if i < 4 else send_ref
            coef = coef_ref[i * PATCHES : (i + 1) * PATCHES, :]
            out_ref[i % 4, :, KV_WIDTH:] = in_two(jnp.where(live, coef, 0.0))


def in_two(coef):
    first = coef.astype(jnp.bfloat16).astype(jnp.float32)
    return (first + pltpu.roll(coef - first, COEFS, 1)).astype(jnp.bfloat16)


def from_two(pair):
    pair = pair.astype(jnp.float32)
    lane = lax.broadcasted_iota(jnp.int32, pair.shape, 1)
    return jnp.where(lane < COEFS, pair + pltpu.roll(pair, COEFS, 1), 0.0)


def backward(meta, stat, q, direction, p, att, inv, images):
    whole = pl.BlockSpec((PATCHES, KV_WIDTH), lambda h: (0, 0))
    rows = GROUP_HEADS * HEAD_DIM
    half = jax.ShapeDtypeStruct((4, PATCHES, WIDE), jnp.bfloat16)
    return pl.pallas_call(
        backward_kernel,
        grid=(KV_HEADS,),
        in_specs=[
            pl.BlockSpec(memory_space=SMEM),
            pl.BlockSpec((8, CAP_LEN), lambda h: (0, 0)),
            pl.BlockSpec((CAP_LEN, rows), lambda h: (0, h)),
            pl.BlockSpec((GROUP_HEADS, HEAD_DIM), lambda h: (h, 0)),
            pl.BlockSpec((GROUP_HEADS, IMG_SLOTS, CAP_LEN), lambda h: (h, 0, 0)),
            pl.BlockSpec((rows, CAP_LEN), lambda h: (h, 0)),
            pl.BlockSpec((GROUP_HEADS, CAP_LEN), lambda h: (h, 0)),
        ]
        + [whole] * CAPS,
        out_specs=[pl.BlockSpec((4, PATCHES, WIDE), lambda h: (0, 0, 0))] * 2,
        out_shape=[half, half],
        scratch_shapes=[VMEM((IMG_SLOTS, HEAD_DIM), jnp.float32)],
        compiler_params=pltpu.CompilerParams(vmem_limit_bytes=VMEM_LIMIT),
        cost_estimate=pl.CostEstimate(
            flops=5_000_000_000, bytes_accessed=28_000_000, transcendentals=0
        ),
        name="backward",
    )(meta, stat, q, direction, p, att, inv, *images)


def scaled_sum_kernel(meta_ref, keep_ref, recv_ref, *rest):
    rewards = rest[:CAPS]
    own_ref, z1_ref, z2_ref, z3_ref, loss_ref = rest[CAPS:]
    place = meta_ref[AT_PLACE]
    lane = lax.broadcasted_iota(jnp.int32, (8, 128), 1)
    sub = lax.broadcasted_iota(jnp.int32, (8, 128), 0)
    by_lane = jnp.zeros((8, 128), jnp.float32)
    by_sub = jnp.zeros((8, 128), jnp.float32)
    for rel in range(CAPS):
        value = rewards[rel][...]
        by_lane = jnp.where(lane == (place ^ rel), value, by_lane)
        by_sub = jnp.where(sub == (place ^ rel), value, by_sub)
    rank_lane = jnp.full((8, 128), CAPS, jnp.int32)
    rank_sub = jnp.zeros((8, 128), jnp.int32)
    for k in range(CAPS):
        who = meta_ref[AT_RANKING + k]
        rank_lane = jnp.where(lane == who, k, rank_lane)
        rank_sub = jnp.where(sub == who, k, rank_sub)
    real = lane < CAPS
    better = real & (rank_sub < rank_lane)
    worse = real & (rank_sub > rank_lane)
    margin = by_lane - by_sub
    soft = jnp.maximum(margin, 0.0) + jnp.log1p(jnp.exp(-jnp.abs(margin)))
    pairs = jnp.where(better, soft, 0.0)
    loss = jnp.sum(jnp.sum(pairs, axis=0, keepdims=True), axis=1, keepdims=True)
    loss_ref[...] = jnp.broadcast_to(loss, (8, 128))
    up = 1.0 / (1.0 + jnp.exp(margin))
    down = 1.0 / (1.0 + jnp.exp(-margin))
    grads = jnp.where(worse, up, 0.0) - jnp.where(better, down, 0.0)
    grads = jnp.sum(grads, axis=1, keepdims=True) * loss_scale
    sub_col = sub[:, :1]
    mine = jnp.sum(jnp.where(sub_col == place, grads, 0.0), axis=0, keepdims=True)
    other = jnp.sum(jnp.where(sub_col == (place ^ 1), grads, 0.0), axis=0, keepdims=True)
    for i, out_ref in enumerate((own_ref, z1_ref, z2_ref, z3_ref)):
        kept, sent = keep_ref[i], recv_ref[i]
        total = kept[:, :KV_WIDTH].astype(jnp.float32) * mine
        total = total + sent[:, :KV_WIDTH].astype(jnp.float32) * other
        coef = from_two(kept[:, KV_WIDTH:]) * mine + from_two(sent[:, KV_WIDTH:]) * other
        out_ref[:, :KV_WIDTH] = total.astype(out_ref.dtype)
        out_ref[:, KV_WIDTH:] = coef if i == 0 else in_two(coef)


def scaled_sum(meta, keep, recv, rewards):
    vmem = pl.BlockSpec(memory_space=VMEM)
    wire = jax.ShapeDtypeStruct((PATCHES, WIDE), jnp.bfloat16)
    return pl.pallas_call(
        scaled_sum_kernel,
        in_specs=[pl.BlockSpec(memory_space=SMEM)] + [vmem] * (2 + CAPS),
        out_specs=[vmem] * 5,
        out_shape=[
            jax.ShapeDtypeStruct((PATCHES, WIDE), jnp.float32),
            wire,
            wire,
            wire,
            jax.ShapeDtypeStruct((8, 128), jnp.float32),
        ],
        compiler_params=pltpu.CompilerParams(vmem_limit_bytes=VMEM_LIMIT),
        name="scaled_sum",
    )(meta, keep, recv, *rewards)


def sum_kernel(own_ref, a_ref, b_ref, c_ref, dir_ref, *rest):
    losses, (out_ref, loss_ref) = rest[:2], rest[2:]
    own = own_ref[...]
    total, coef = own[:, :KV_WIDTH], own[:, KV_WIDTH:]
    for part in (a_ref, b_ref, c_ref):
        total = total + part[:, :KV_WIDTH].astype(jnp.float32)
        coef = coef + from_two(part[:, KV_WIDTH:])
    out_ref[:, : KV_WIDTH // 2] = total[:, : KV_WIDTH // 2].astype(out_ref.dtype)
    for head in range(KV_HEADS):
        cols = slice((KV_HEADS + head) * HEAD_DIM, (KV_HEADS + head + 1) * HEAD_DIM)
        value = total[:, cols]
        for j in range(head * GROUP_HEADS, (head + 1) * GROUP_HEADS):
            value = value + coef[:, j : j + 1] * dir_ref[j : j + 1, :]
        out_ref[:, cols] = value.astype(out_ref.dtype)
    loss_ref[...] = losses[0][...] + losses[1][...]


def group_sum(own, parts, direction, losses):
    vmem = pl.BlockSpec(memory_space=VMEM)
    return pl.pallas_call(
        sum_kernel,
        in_specs=[vmem] * 7,
        out_specs=[vmem] * 2,
        out_shape=[
            jax.ShapeDtypeStruct((PATCHES, KV_WIDTH), jnp.bfloat16),
            jax.ShapeDtypeStruct((8, 128), jnp.float32),
        ],
        name="group_sum",
    )(own, *parts, direction, *losses)


def sort_kernel(meta_ref, s0, s1, s2, s3, l0, l1, keep_ref, send_ref, loss_ref):
    total = jnp.zeros((PATCHES, KV_WIDTH), jnp.float32)
    kept = jnp.zeros((PATCHES, KV_WIDTH), jnp.float32)
    for k, part in enumerate((s0, s1, s2, s3)):
        dest = meta_ref[AT_DEST + k]
        value = part[...].astype(jnp.float32)
        kept = kept + jnp.where(dest == 1, value, 0.0)
        total = total + jnp.where(dest == 2, value, 0.0)
    keep_ref[...] = kept
    send_ref[...] = total.astype(send_ref.dtype)
    loss_ref[...] = l0[...] + l1[...]


def sort_by_owner(meta, parts, losses):
    vmem = pl.BlockSpec(memory_space=VMEM)
    return pl.pallas_call(
        sort_kernel,
        in_specs=[pl.BlockSpec(memory_space=SMEM)] + [vmem] * 6,
        out_specs=[vmem] * 3,
        out_shape=[
            jax.ShapeDtypeStruct((PATCHES, KV_WIDTH), jnp.float32),
            jax.ShapeDtypeStruct((PATCHES, KV_WIDTH), jnp.bfloat16),
            jax.ShapeDtypeStruct((8, 128), jnp.float32),
        ],
        name="sort_by_owner",
    )(meta, *parts, *losses)


def along_y(value, step):
    pairs = [(s, s // 4 * 4 + (s + step) % 4) for s in range(8)]
    return lax.ppermute(value, "segment", pairs)


def across(value, axis, mask):
    size = lax.axis_size(axis)
    return lax.ppermute(value, axis, [(i, i ^ mask) for i in range(size)])


def per_device(
    queries, caption_kv, caption_len, image_kv, patch_count, image_list, pref_order, reward_dir
):
    idx = jnp.stack([lax.axis_index("segment"), lax.axis_index("tp")]).astype(jnp.int32)
    image = image_kv[0]
    q = queries[0]
    direction = reward_dir.reshape(KV_HEADS * GROUP_HEADS, HEAD_DIM)
    meta = make_meta(idx, image_list, patch_count, pref_order, caption_len)

    column = [image] + [along_y(image, step) for step in (1, 2, 3)]
    far = across(pick(pick_partner_kernel, "pick_partner", meta, *column), "segment", 4)
    own = pick(pick_own_kernel, "pick_own", meta, *column, far)
    same_core = [own] + [across(own, "tp", mask) for mask in (2, 4, 6)]
    images = same_core + [across(one, "tp", 1) for one in same_core]

    p, att, inv, stat, reward = forward(meta, q, caption_kv[0], direction, images)
    rewards = [reward] + [across(reward, "tp", mask) for mask in range(1, CAPS)]
    keep, send = backward(meta, stat, q, direction, p, att, inv, images)
    recv = across(send, "tp", 1)
    mine, to_z1, to_z2, to_z3, loss = scaled_sum(meta, keep, recv, rewards)
    parts = [across(to_z1, "tp", 2), across(to_z2, "tp", 4), across(to_z3, "tp", 6)]
    loss = loss + across(loss, "tp", 8)
    total, loss = group_sum(mine, parts, direction, (loss, across(loss, "tp", 16)))
    totals = [total] + [along_y(total, step) for step in (1, 2, 3)]
    loss = loss + across(loss, "segment", 1)
    kept, away, loss = sort_by_owner(meta, totals, (loss, across(loss, "segment", 2)))
    loss = loss + across(loss, "segment", 4)
    image_grad = kept + across(away, "segment", 4).astype(jnp.float32)
    return (loss[0, 0], reward[0, :1], image_grad[None])


def solution(mesh):
    placed = (
        P(("segment", "tp"), None, None),
        P(("segment", "tp"), None, None),
        P(("segment", "tp")),
        P(("segment", "tp"), None, None),
        P(),
        P(),
        P(),
        P(),
    )
    return jax.shard_map(
        per_device,
        mesh=mesh,
        in_specs=placed,
        out_specs=(P(), P(("segment", "tp")), P(("segment", "tp"), None, None)),
        check_vma=False,
    )
```

```python
import functools
import math

import jax
import jax.numpy as jnp
from jax import lax
from jax.experimental import pallas as pl
from jax.experimental.pallas import tpu as pltpu
from jax.sharding import PartitionSpec as P

D = 8192
KV_HEADS = 8
HEAD_DIM = 128
CAP_LEN = 256
PATCHES = 48
CAPS = 8
GROUP_HEADS = 8
KV_WIDTH = 2048
COLUMNS = 32
IMG_SLOTS = CAPS * PATCHES
COEFS = KV_HEADS * GROUP_HEADS
WIDE = KV_WIDTH + 2 * COEFS
HALF = CAP_LEN // 2

norm_eps = 1e-06
loss_scale = 65536.0
scaling = 1.0 / math.sqrt(HEAD_DIM)
to_base2 = scaling * math.log2(math.e)

SMEM = pltpu.SMEM
VMEM = pltpu.VMEM
VMEM_LIMIT = 16 * 1024 * 1024
BIG_LIMIT = 56 * 1024 * 1024

AT_Y, AT_SRC_Y, AT_SRC_X_SAME, AT_PARTNER_Y, AT_PLACE, AT_LEN = 0, 1, 2, 3, 4, 5
AT_COUNTS, AT_RANKING, AT_DEST = 8, 16, 24

REL = (0, 2, 4, 6, 1, 3, 5, 7)

SUM_HIGH = 2.0**60
TOGETHER = 2


def exact_dot(a, b, dims):
    return lax.dot_general(a, b, (dims, ((), ())), preferred_element_type=jnp.float32)


def meta_kernel(idx_ref, list_ref, count_ref, order_ref, len_ref, out_ref):
    seg = idx_ref[0]
    col = idx_ref[1]
    x = seg // 4
    y = seg % 4
    slot = col // CAPS
    place = col % CAPS

    def section_of(section):
        return list_ref[section * 4 + slot, place] // COLUMNS

    own = section_of(seg)
    partner = section_of((1 - x) * 4 + y)
    out_ref[AT_Y] = y
    out_ref[AT_SRC_Y] = own % 4
    out_ref[AT_SRC_X_SAME] = (own // 4 == x).astype(jnp.int32)
    out_ref[AT_PARTNER_Y] = partner % 4
    out_ref[AT_PLACE] = place
    out_ref[AT_LEN] = len_ref[0]
    group = seg * 4 + slot
    for i, rel in enumerate(REL):
        out_ref[AT_COUNTS + i] = count_ref[list_ref[group, place ^ rel]]
    for k in range(CAPS):
        out_ref[AT_RANKING + k] = order_ref[group, k]
    for k in range(4):
        dest = section_of(x * 4 + (y + 4 - k) % 4)
        here = (dest % 4 == y).astype(jnp.int32)
        out_ref[AT_DEST + k] = here * jnp.where(dest // 4 == x, 1, 2)


def make_meta(idx, image_list, patch_count, pref_order, caption_len):
    smem = pl.BlockSpec(memory_space=SMEM)
    return pl.pallas_call(
        meta_kernel,
        out_shape=jax.ShapeDtypeStruct((32,), jnp.int32),
        in_specs=[smem] * 5,
        out_specs=smem,
        name="meta",
    )(idx, image_list, patch_count, pref_order, caption_len)


def pick_partner_kernel(meta_ref, i0, i1, i2, i3, out_ref, sem):
    y = meta_ref[AT_Y]
    back = (y + 4 - meta_ref[AT_PARTNER_Y]) % 4
    for k, src in enumerate((i0, i1, i2, i3)):

        @pl.when(back == k)
        def _():
            copy = pltpu.make_async_copy(src, out_ref, sem)
            copy.start()
            copy.wait()


def pick_own_kernel(meta_ref, i0, i1, i2, i3, far, out_ref, sem):
    y = meta_ref[AT_Y]
    same = meta_ref[AT_SRC_X_SAME]
    back = jnp.where(same == 1, (y + 4 - meta_ref[AT_SRC_Y]) % 4, 4)
    for k, src in enumerate((i0, i1, i2, i3, far)):

        @pl.when(back == k)
        def _():
            copy = pltpu.make_async_copy(src, out_ref, sem)
            copy.start()
            copy.wait()


def pick(kernel, name, meta, *images):
    any_space = pl.BlockSpec(memory_space=pl.ANY)
    return pl.pallas_call(
        kernel,
        out_shape=jax.ShapeDtypeStruct(images[0].shape, images[0].dtype),
        in_specs=[pl.BlockSpec(memory_space=SMEM)] + [any_space] * len(images),
        out_specs=pl.BlockSpec(memory_space=VMEM),
        scratch_shapes=[pltpu.SemaphoreType.DMA],
        name=name,
    )(meta, *images)


def head_columns(head):
    keys = pl.ds(pl.multiple_of(head * HEAD_DIM, HEAD_DIM), HEAD_DIM)
    values = pl.ds(pl.multiple_of((KV_HEADS + head) * HEAD_DIM, HEAD_DIM), HEAD_DIM)
    return keys, values


def with_marks(values, marks):
    values_t = jnp.concatenate(values, axis=0).T
    marks_t = jnp.concatenate(marks, axis=0).T[:16]
    return jnp.concatenate([values_t, marks_t], axis=0).astype(jnp.bfloat16)


def pipelined(count, start, finish):
    ahead = start(0)
    done = []
    for g in range(count):
        now = ahead
        if g + 1 < count:
            ahead = start(g + 1)
        done.append(finish(g, now))
    return done


def column(g):
    return slice(g * HEAD_DIM, (g + 1) * HEAD_DIM)


def own_kernel(q_ref, key_ref, value_ref, acc_ref, max_ref, sum_ref):
    keys = key_ref[...]
    mixed = with_marks(
        [value_ref[...].astype(jnp.float32)], [jnp.ones((CAP_LEN, HEAD_DIM), jnp.float32)]
    )
    diagonal = lax.broadcasted_iota(jnp.int32, (HALF, HALF), 0) <= lax.broadcasted_iota(
        jnp.int32, (HALF, HALF), 1
    )
    minus = jnp.full((HALF, HALF), -jnp.inf, jnp.float32)

    def start(g):
        return exact_dot(keys, q_ref[:, column(g)], ((1,), (1,)))

    def finish(g, s):
        s_a = jnp.where(diagonal, s[:HALF, :HALF], minus)
        s_b = s[:HALF, HALF:]
        s_c = jnp.where(diagonal, s[HALF:, HALF:], minus)
        m_low = jnp.max(s_a, axis=0, keepdims=True) * to_base2
        m_high = jnp.max(jnp.maximum(s_b, s_c), axis=0, keepdims=True) * to_base2
        p_a = jnp.exp2(s_a * to_base2 - m_low).astype(jnp.bfloat16)
        p_b = jnp.exp2(s_b * to_base2 - m_high).astype(jnp.bfloat16)
        p_c = jnp.exp2(s_c * to_base2 - m_high).astype(jnp.bfloat16)
        p = jnp.concatenate(
            [
                jnp.concatenate([p_a, p_b], axis=1),
                jnp.concatenate([jnp.zeros_like(p_c), p_c], axis=1),
            ],
            axis=0,
        )
        out = exact_dot(mixed, p, ((1,), (0,)))
        acc_ref[column(g), :] = out[:HEAD_DIM]
        max_ref[g : g + 1, :] = jnp.concatenate([m_low, m_high], axis=1)
        sum_ref[g : g + 1, :] = out[HEAD_DIM : HEAD_DIM + 1]

    pipelined(GROUP_HEADS, start, finish)


def image_parts(meta_ref, images, key_cols, value_cols):
    row = lax.broadcasted_iota(jnp.int32, (PATCHES, HEAD_DIM), 0)
    keys, values, marks = [], [], []
    for i, image in enumerate(images):
        live = row < meta_ref[AT_COUNTS + i]
        key = image[:, key_cols].astype(jnp.float32)
        keys.append(jnp.where(live, key, key[0:1, :]).astype(jnp.bfloat16))
        values.append(jnp.where(live, image[:, value_cols].astype(jnp.float32), 0.0))
        marks.append(live.astype(jnp.float32))
    return jnp.concatenate(keys, axis=0), with_marks(values, marks)


def forward_step(head, meta_ref, q_ref, dir_ref, state, images, kept, stat_ref, reward_ref, sum_refs):
    acc_in, max_in, sum_in = state
    p_ref, att_ref, inv_ref = kept
    ss_ref, rd_ref = sum_refs
    keys, mixed = image_parts(meta_ref, images, *head_columns(head))
    dir_t = dir_ref[...].T

    @pl.when(head == 0)
    def _():
        ss_ref[...] = jnp.zeros_like(ss_ref)
        rd_ref[...] = jnp.zeros_like(rd_ref)

    def start(g):
        return exact_dot(keys, q_ref[:, column(g)], ((1,), (1,)))

    def attended(p, acc, total):
        out = exact_dot(mixed, p, ((1,), (0,)))
        total = total + out[HEAD_DIM : HEAD_DIM + 1]
        return (acc + out[:HEAD_DIM]) * (1.0 / total), total

    def square_and_reward(att, dir_col):
        ss = jnp.sum((att * att).reshape(16, 8, CAP_LEN), axis=0)
        return ss, jnp.sum((att * dir_col).reshape(16, 8, CAP_LEN), axis=0)

    zero = jnp.zeros((8, CAP_LEN), jnp.float32)
    sums = [zero, zero, jnp.zeros((1, CAP_LEN), jnp.float32)]

    def finish(g, s):
        p = jnp.exp2(s * to_base2 - max_in[g : g + 1, :]).astype(jnp.bfloat16)
        p_ref[g] = p
        att, total = attended(p, acc_in[column(g), :], sum_in[g : g + 1, :])
        att_ref[column(g), :] = att
        inv_ref[g : g + 1, :] = 1.0 / total
        ss, rd = square_and_reward(att, dir_t[:, g : g + 1])
        sums[0] += ss
        sums[1] += rd
        sums[2] = jnp.maximum(sums[2], total)

    pipelined(GROUP_HEADS, start, finish)
    inside = jnp.max(sums[2]) < SUM_HIGH

    @pl.when(inside)
    def _():
        ss_ref[...] += sums[0]
        rd_ref[...] += sums[1]

    @pl.when(jnp.logical_not(inside))
    def _():
        for g in range(GROUP_HEADS):
            s = start(g)
            old = max_in[g : g + 1, :]
            new = jnp.maximum(old, jnp.max(s, axis=0, keepdims=True) * to_base2)
            shrink = jnp.exp2(old - new)
            p = jnp.exp2(s * to_base2 - new).astype(jnp.bfloat16)
            p_ref[g] = p
            att, total = attended(p, acc_in[column(g), :] * shrink, sum_in[g : g + 1, :] * shrink)
            att_ref[column(g), :] = att
            inv_ref[g : g + 1, :] = 1.0 / total
            ss, rd = square_and_reward(att, dir_t[:, g : g + 1])
            ss_ref[...] += ss
            rd_ref[...] += rd

    @pl.when(head == KV_HEADS - 1)
    def _():
        ss = ss_ref[...]
        rd = rd_ref[...]
        length = meta_ref[AT_LEN]
        inv_rms = lax.rsqrt(jnp.sum(ss, axis=0, keepdims=True) * (1.0 / D) + norm_eps)
        per_token = jnp.sum(rd, axis=0, keepdims=True) * inv_rms
        live = lax.broadcasted_iota(jnp.int32, (1, CAP_LEN), 1) < length
        length_f = jnp.full((1, CAP_LEN), length, jnp.int32).astype(jnp.float32)
        unit = jnp.where(live, 1.0 / length_f, 0.0)
        a = inv_rms * unit
        b = inv_rms * inv_rms * unit * per_token * (1.0 / D)
        stat_ref[...] = jnp.concatenate([a, b, jnp.zeros((6, CAP_LEN), jnp.float32)], axis=0)
        reward = jnp.sum(jnp.where(live, per_token, 0.0), axis=1, keepdims=True)
        reward_ref[...] = jnp.broadcast_to(reward / length_f[:, :1], (8, 128))


ROWS = GROUP_HEADS * HEAD_DIM
Q_SPEC = pl.BlockSpec((CAP_LEN, ROWS), lambda h: (0, h))
ACC_SPEC = pl.BlockSpec((ROWS, CAP_LEN), lambda h: (h, 0))
ROW_SPEC = pl.BlockSpec((GROUP_HEADS, CAP_LEN), lambda h: (h, 0))
SMEM_SPEC = pl.BlockSpec(memory_space=SMEM)
ACC = jax.ShapeDtypeStruct((D, CAP_LEN), jnp.float32)
ROW = jax.ShapeDtypeStruct((COEFS, CAP_LEN), jnp.float32)
TILE = jax.ShapeDtypeStruct((8, 128), jnp.float32)


def by_head(kernel, name, in_specs, out_specs, out_shape, scratch=(), flops=2_000_000_000):
    return pl.pallas_call(
        kernel,
        grid=(KV_HEADS,),
        in_specs=in_specs,
        out_specs=out_specs,
        out_shape=out_shape,
        scratch_shapes=scratch,
        compiler_params=pltpu.CompilerParams(vmem_limit_bytes=BIG_LIMIT),
        cost_estimate=pl.CostEstimate(
            flops=flops, bytes_accessed=16_000_000, transcendentals=4_000_000
        ),
        name=name,
    )


def attend_own(q, own_kv):
    key = pl.BlockSpec((CAP_LEN, HEAD_DIM), lambda h: (0, h))
    value = pl.BlockSpec((CAP_LEN, HEAD_DIM), lambda h: (0, KV_HEADS + h))
    call = by_head(
        own_kernel, "attend_own", [Q_SPEC, key, value], [ACC_SPEC, ROW_SPEC, ROW_SPEC], [ACC, ROW, ROW]
    )
    return call(q, own_kv, own_kv)


def backward_step(head, meta_ref, q_ref, dir_ref, images, kept, stat_ref, outs, coef_ref):
    p_ref, att_ref, inv_ref = kept
    keep_ref, send_ref = outs
    key_cols, value_cols = head_columns(head)
    values = jnp.concatenate([image[:, value_cols] for image in images], axis=0)
    dir_t = dir_ref[...].T
    a = stat_ref[0:1, :]
    b = stat_ref[1:2, :]
    which = lax.broadcasted_iota(jnp.int32, (HEAD_DIM, CAP_LEN), 0)

    @pl.when(head == 0)
    def _():
        coef_ref[...] = jnp.zeros_like(coef_ref)

    key_grad = jnp.zeros((IMG_SLOTS, HEAD_DIM), jnp.float32)
    value_grad = jnp.zeros((IMG_SLOTS, 2 * HEAD_DIM), jnp.float32)

    def start(g):
        att = att_ref[column(g), :]
        inv = inv_ref[g : g + 1, :]
        factor = a * inv
        rest_grad = -(b * inv) * att
        grad = (factor * dir_t[:, g : g + 1] + rest_grad).astype(jnp.bfloat16)
        delta = jnp.sum(grad.astype(jnp.float32) * att, axis=0, keepdims=True)
        factors = jnp.where(which == head * GROUP_HEADS + g, factor, 0.0)
        apart = jnp.concatenate([rest_grad, factors], axis=0).astype(jnp.bfloat16)
        return exact_dot(values, grad, ((1,), (0,))), delta, apart

    def finish(g, started):
        weight_grad, delta, apart = started
        p = p_ref[g]
        return p, (p.astype(jnp.float32) * (weight_grad - delta)).astype(jnp.bfloat16), apart

    for first in range(0, GROUP_HEADS, TOGETHER):
        done = pipelined(TOGETHER, lambda g: start(first + g), lambda g, x: finish(first + g, x))
        p, score_grad, apart = (jnp.concatenate(part, axis=1) for part in zip(*done))
        q = jnp.concatenate([q_ref[:, column(first + g)] for g in range(TOGETHER)], axis=0)
        value_grad = value_grad + exact_dot(p, apart, ((1,), (1,)))
        key_grad = key_grad + exact_dot(score_grad, q, ((1,), (0,)))
    key_grad = key_grad * scaling
    row = lax.broadcasted_iota(jnp.int32, (PATCHES, HEAD_DIM), 0)
    for i in range(CAPS):
        live = row < meta_ref[AT_COUNTS + i]
        out_ref = keep_ref if i < 4 else send_ref
        part = slice(i * PATCHES, (i + 1) * PATCHES)
        out_ref[i % 4, :, key_cols] = jnp.where(live, key_grad[part], 0.0).astype(jnp.bfloat16)
        out_ref[i % 4, :, value_cols] = jnp.where(
            live, value_grad[part, :HEAD_DIM], 0.0
        ).astype(jnp.bfloat16)
    coef_ref[...] += value_grad[:, HEAD_DIM:]

    @pl.when(head == KV_HEADS - 1)
    def _():
        for i in range(CAPS):
            live = row < meta_ref[AT_COUNTS + i]
            out_ref = keep_ref if i < 4 else send_ref
            coef = coef_ref[i * PATCHES : (i + 1) * PATCHES, :]
            out_ref[i % 4, :, KV_WIDTH:] = in_two(jnp.where(live, coef, 0.0))


def in_two(coef):
    first = coef.astype(jnp.bfloat16).astype(jnp.float32)
    return (first + pltpu.roll(coef - first, COEFS, 1)).astype(jnp.bfloat16)


def from_two(pair):
    pair = pair.astype(jnp.float32)
    lane = lax.broadcasted_iota(jnp.int32, pair.shape, 1)
    return jnp.where(lane < COEFS, pair + pltpu.roll(pair, COEFS, 1), 0.0)


def image_kernel(meta_ref, q_ref, dir_ref, acc_in, max_in, sum_in, *rest):
    images = rest[:CAPS]
    keep_ref, send_ref, reward_ref = rest[CAPS : CAPS + 3]
    p_all, att_all, inv_all, stat_ref, ss_ref, rd_ref, coef_ref = rest[CAPS + 3 :]
    step = pl.program_id(0)
    head = step % KV_HEADS
    kept = (p_all.at[head], att_all.at[head], inv_all.at[head])

    @pl.when(step < KV_HEADS)
    def _():
        state = (acc_in, max_in, sum_in)
        sums = (ss_ref, rd_ref)
        forward_step(
            head, meta_ref, q_ref, dir_ref, state, images, kept, stat_ref, reward_ref, sums
        )

    @pl.when(step >= KV_HEADS)
    def _():
        outs = (keep_ref, send_ref)
        backward_step(head, meta_ref, q_ref, dir_ref, images, kept, stat_ref, outs, coef_ref)


def attend_images(meta, q, direction, state, images):
    half = jax.ShapeDtypeStruct((4, PATCHES, WIDE), jnp.bfloat16)
    half_spec = pl.BlockSpec((4, PATCHES, WIDE), lambda s: (0, 0, 0))

    def once(s):
        return (jnp.minimum(s, KV_HEADS - 1), 0)

    row_spec = pl.BlockSpec((GROUP_HEADS, CAP_LEN), once)
    call = pl.pallas_call(
        image_kernel,
        grid=(2 * KV_HEADS,),
        in_specs=[
            SMEM_SPEC,
            pl.BlockSpec((CAP_LEN, ROWS), lambda s: (0, s % KV_HEADS)),
            pl.BlockSpec((GROUP_HEADS, HEAD_DIM), lambda s: (s % KV_HEADS, 0)),
            pl.BlockSpec((ROWS, CAP_LEN), once),
            row_spec,
            row_spec,
        ]
        + [pl.BlockSpec((PATCHES, KV_WIDTH), lambda s: (0, 0))] * CAPS,
        out_specs=[half_spec, half_spec, pl.BlockSpec((8, 128), lambda s: (0, 0))],
        out_shape=[half, half, TILE],
        scratch_shapes=[
            VMEM((KV_HEADS, GROUP_HEADS, IMG_SLOTS, CAP_LEN), jnp.bfloat16),
            VMEM((KV_HEADS, ROWS, CAP_LEN), jnp.float32),
            VMEM((KV_HEADS, GROUP_HEADS, CAP_LEN), jnp.float32),
            VMEM((8, CAP_LEN), jnp.float32),
            VMEM((8, CAP_LEN), jnp.float32),
            VMEM((8, CAP_LEN), jnp.float32),
            VMEM((IMG_SLOTS, HEAD_DIM), jnp.float32),
        ],
        compiler_params=pltpu.CompilerParams(vmem_limit_bytes=BIG_LIMIT),
        cost_estimate=pl.CostEstimate(
            flops=8_000_000_000, bytes_accessed=18_000_000, transcendentals=6_000_000
        ),
        name="attend_images",
    )
    return call(meta, q, direction, *state, *images)


def group_loss(place, rewards, meta_ref):
    lane = lax.broadcasted_iota(jnp.int32, (8, 128), 1)
    sub = lax.broadcasted_iota(jnp.int32, (8, 128), 0)
    by_lane = jnp.zeros((8, 128), jnp.float32)
    by_sub = jnp.zeros((8, 128), jnp.float32)
    for rel in range(CAPS):
        tile = rewards[rel // 2][...]
        value = jnp.where((place ^ rel) % 2 == 0, tile[0:1, :], tile[1:2, :])
        by_lane = jnp.where(lane == (place ^ rel), value, by_lane)
        by_sub = jnp.where(sub == (place ^ rel), value, by_sub)
    rank_lane = jnp.full((8, 128), CAPS, jnp.int32)
    rank_sub = jnp.zeros((8, 128), jnp.int32)
    for k in range(CAPS):
        who = meta_ref[AT_RANKING + k]
        rank_lane = jnp.where(lane == who, k, rank_lane)
        rank_sub = jnp.where(sub == who, k, rank_sub)
    real = lane < CAPS
    better = real & (rank_sub < rank_lane)
    worse = real & (rank_sub > rank_lane)
    margin = by_lane - by_sub
    soft = jnp.maximum(margin, 0.0) + jnp.log1p(jnp.exp(-jnp.abs(margin)))
    pairs = jnp.where(better, soft, 0.0)
    loss = jnp.sum(jnp.sum(pairs, axis=0, keepdims=True), axis=1, keepdims=True)
    up = 1.0 / (1.0 + jnp.exp(margin))
    down = 1.0 / (1.0 + jnp.exp(-margin))
    grads = jnp.where(worse, up, 0.0) - jnp.where(better, down, 0.0)
    grads = jnp.sum(grads, axis=1, keepdims=True) * loss_scale
    sub_col = sub[:, :1]
    mine = jnp.sum(jnp.where(sub_col == place, grads, 0.0), axis=0, keepdims=True)
    other = jnp.sum(jnp.where(sub_col == (place ^ 1), grads, 0.0), axis=0, keepdims=True)
    return loss, mine, other


def scaled_sum_kernel(meta_ref, keep_ref, recv_ref, *rest):
    rewards = rest[:4]
    *outs, loss_ref = rest[4:]
    loss, mine, other = group_loss(meta_ref[AT_PLACE], rewards, meta_ref)
    loss_ref[...] = jnp.broadcast_to(loss, (8, 128))
    for i, out_ref in enumerate(outs):
        kept, sent = keep_ref[i], recv_ref[i]
        total = kept[:, :KV_WIDTH].astype(jnp.float32) * mine
        total = total + sent[:, :KV_WIDTH].astype(jnp.float32) * other
        coef = from_two(kept[:, KV_WIDTH:]) * mine + from_two(sent[:, KV_WIDTH:]) * other
        out_ref[:, :KV_WIDTH] = total.astype(out_ref.dtype)
        wide = out_ref.dtype == jnp.float32
        out_ref[:, KV_WIDTH:] = coef if wide else in_two(coef)


def in_vmem(kernel, name, count, out_shape, meta=True):
    vmem = pl.BlockSpec(memory_space=VMEM)
    return pl.pallas_call(
        kernel,
        in_specs=[SMEM_SPEC] * meta + [vmem] * count,
        out_specs=[vmem] * len(out_shape),
        out_shape=out_shape,
        compiler_params=pltpu.CompilerParams(vmem_limit_bytes=VMEM_LIMIT),
        name=name,
    )


WIRE = jax.ShapeDtypeStruct((PATCHES, WIDE), jnp.bfloat16)
TOTAL = jax.ShapeDtypeStruct((PATCHES, WIDE), jnp.float32)


def scaled_sum(meta, keep, recv, rewards):
    outs = [TOTAL, WIRE, WIRE, WIRE, TILE]
    call = in_vmem(scaled_sum_kernel, "scaled_sum", 6, outs)
    return call(meta, keep, recv, *rewards)


def in_three(value):
    terms = []
    for _ in range(3):
        term = value.astype(jnp.bfloat16).astype(jnp.float32)
        terms.append(term)
        value = value - term
    return terms


def store_loss(ref, loss):
    lane = lax.broadcasted_iota(jnp.int32, (PATCHES, 128), 1)
    first, second, third = (term[:1] for term in in_three(loss))
    row = jnp.where(lane == 0, first, jnp.where(lane == 1, second, third))
    ref[:, KV_WIDTH:] = row.astype(jnp.bfloat16)


def read_loss(ref):
    row = ref[:8, KV_WIDTH:].astype(jnp.float32)
    return jnp.broadcast_to(row[:, 0:1] + row[:, 1:2] + row[:, 2:3], (8, 128))


def sum_kernel(own_ref, a_ref, b_ref, c_ref, dir_ref, l0_ref, l1_ref, out_ref):
    own = own_ref[...]
    total, coef = own[:, :KV_WIDTH], own[:, KV_WIDTH:]
    for part in (a_ref, b_ref, c_ref):
        total = total + part[:, :KV_WIDTH].astype(jnp.float32)
        coef = coef + from_two(part[:, KV_WIDTH:])
    out_ref[:, : KV_WIDTH // 2] = total[:, : KV_WIDTH // 2].astype(out_ref.dtype)
    for head in range(KV_HEADS):
        cols = column(KV_HEADS + head)
        value = total[:, cols]
        for j in range(head * GROUP_HEADS, (head + 1) * GROUP_HEADS):
            value = value + coef[:, j : j + 1] * dir_ref[j : j + 1, :]
        out_ref[:, cols] = value.astype(out_ref.dtype)
    store_loss(out_ref, l0_ref[...] + l1_ref[...])


def group_sum(own, parts, direction, losses):
    call = in_vmem(sum_kernel, "group_sum", 7, [WIRE], meta=False)
    return call(own, *parts, direction, *losses)[0]


def sort_kernel(meta_ref, s0, s1, s2, s3, keep_ref, send_ref, loss_ref):
    total = jnp.zeros((PATCHES, KV_WIDTH), jnp.float32)
    kept = jnp.zeros((PATCHES, KV_WIDTH), jnp.float32)
    for k, part in enumerate((s0, s1, s2, s3)):
        dest = meta_ref[AT_DEST + k]
        value = part[:, :KV_WIDTH].astype(jnp.float32)
        kept = kept + jnp.where(dest == 1, value, 0.0)
        total = total + jnp.where(dest == 2, value, 0.0)
    keep_ref[...] = kept
    send_ref[:, :KV_WIDTH] = total.astype(send_ref.dtype)
    loss = (read_loss(s0) + read_loss(s2)) + (read_loss(s1) + read_loss(s3))
    store_loss(send_ref, loss)
    loss_ref[...] = loss


def sort_by_owner(meta, parts):
    grad = jax.ShapeDtypeStruct((PATCHES, KV_WIDTH), jnp.float32)
    return in_vmem(sort_kernel, "sort_by_owner", 4, [grad, WIRE, TILE])(meta, *parts)


def last_kernel(keep_ref, recv_ref, l0_ref, l2_ref, l3_ref, out_ref, loss_ref):
    out_ref[0] = keep_ref[...] + recv_ref[:, :KV_WIDTH].astype(jnp.float32)
    loss_ref[...] = (l0_ref[...] + read_loss(recv_ref)) + (l2_ref[...] + l3_ref[...])


def last_sum(kept, recv, losses):
    grad = jax.ShapeDtypeStruct((1, PATCHES, KV_WIDTH), jnp.float32)
    call = in_vmem(last_kernel, "last_sum", 5, [grad, TILE], meta=False)
    return call(kept, recv, *losses)


def along_y(value, step):
    pairs = [(s, s // 4 * 4 + (s + step) % 4) for s in range(8)]
    return lax.ppermute(value, "segment", pairs)


def across(value, axis, mask):
    size = lax.axis_size(axis)
    return lax.ppermute(value, axis, [(i, i ^ mask) for i in range(size)])


def per_device(
    queries, caption_kv, caption_len, image_kv, patch_count, image_list, pref_order, reward_dir
):
    idx = jnp.stack([lax.axis_index("segment"), lax.axis_index("tp")]).astype(jnp.int32)
    image = image_kv[0]
    q = queries[0]
    direction = reward_dir.reshape(KV_HEADS * GROUP_HEADS, HEAD_DIM)
    meta = make_meta(idx, image_list, patch_count, pref_order, caption_len)

    seen = [image] + [along_y(image, step) for step in (1, 2, 3)]
    wanted = pick(pick_partner_kernel, "pick_partner", meta, *seen)
    own = pick(pick_own_kernel, "pick_own", meta, *seen, across(wanted, "segment", 4))
    acc, top, total = attend_own(q, caption_kv[0])
    others = [across(own, "tp", mask) for mask in (2, 4, 6)]
    *others, top = lax.optimization_barrier((*others, top))
    same_core = [own, *others]
    images = same_core + [across(one, "tp", 1) for one in same_core]

    keep, send, reward = attend_images(meta, q, direction, (acc, top, total), images)
    recv = across(send, "tp", 1)
    other = across(reward, "tp", 1)
    second = lax.axis_index("tp") % 2 == 1
    row = lax.broadcasted_iota(jnp.int32, reward.shape, 0)
    pair = jnp.where((row == 1) == second, reward, other)
    rewards = [pair] + [across(pair, "tp", mask) for mask in (2, 4, 6)]
    mine, to_z1, to_z2, to_z3, loss = scaled_sum(meta, keep, recv, rewards)
    parts = [across(to_z1, "tp", 2), across(to_z2, "tp", 4), across(to_z3, "tp", 6)]
    total = group_sum(mine, parts, direction, (loss, across(loss, "tp", 8)))
    totals = [total] + [along_y(total, step) for step in (1, 2, 3)]
    kept, away, loss = sort_by_owner(meta, totals)
    both = [(i, i ^ (4 * COLUMNS + 16)) for i in range(8 * COLUMNS)]
    diagonal = lax.ppermute(loss, ("segment", "tp"), both)
    losses = (loss, across(loss, "tp", 16), diagonal)
    image_grad, loss = last_sum(kept, across(away, "segment", 4), losses)
    return (loss[0, 0], reward[0, :1], image_grad)


def solution(mesh):
    placed = (
        P(("segment", "tp"), None, None),
        P(("segment", "tp"), None, None),
        P(("segment", "tp")),
        P(("segment", "tp"), None, None),
        P(),
        P(),
        P(),
        P(),
    )
    return jax.shard_map(
        per_device,
        mesh=mesh,
        in_specs=placed,
        out_specs=(P(), P(("segment", "tp")), P(("segment", "tp"), None, None)),
        check_vma=False,
    )
```

```python
import functools
import math

import jax
import jax.numpy as jnp
from jax import lax
from jax.experimental import pallas as pl
from jax.experimental.pallas import tpu as pltpu
from jax.sharding import PartitionSpec as P

D = 8192
KV_HEADS = 8
HEAD_DIM = 128
CAP_LEN = 256
PATCHES = 48
CAPS = 8
GROUP_HEADS = 8
KV_WIDTH = 2048
COLUMNS = 32
IMG_SLOTS = CAPS * PATCHES
COEFS = KV_HEADS * GROUP_HEADS
WIDE = KV_WIDTH + 2 * COEFS
HALF = CAP_LEN // 2

norm_eps = 1e-06
loss_scale = 65536.0
scaling = 1.0 / math.sqrt(HEAD_DIM)
to_base2 = scaling * math.log2(math.e)

SMEM = pltpu.SMEM
VMEM = pltpu.VMEM
VMEM_LIMIT = 16 * 1024 * 1024
BIG_LIMIT = 56 * 1024 * 1024

AT_FOR_PARTNER, AT_OWN, AT_PLACE, AT_LEN = 0, 1, 2, 3
AT_COUNTS, AT_RANKING, AT_DEST = 8, 16, 24

REL = (0, 2, 4, 6, 1, 3, 5, 7)

SUM_HIGH = 2.0**60


def exact_dot(a, b, dims):
    return lax.dot_general(a, b, (dims, ((), ())), preferred_element_type=jnp.float32)


def meta_kernel(idx_ref, list_ref, count_ref, order_ref, len_ref, out_ref):
    seg = idx_ref[0]
    col = idx_ref[1]
    x = seg // 4
    y = seg % 4
    slot = col // CAPS
    place = col % CAPS

    def section_of(section):
        return list_ref[section * 4 + slot, place] // COLUMNS

    own = section_of(seg)
    partner = section_of((1 - x) * 4 + y)
    out_ref[AT_FOR_PARTNER] = (y + 4 - partner % 4) % 4
    out_ref[AT_OWN] = jnp.where(own // 4 == x, (y + 4 - own % 4) % 4, 4)
    out_ref[AT_PLACE] = place
    out_ref[AT_LEN] = len_ref[0]
    group = seg * 4 + slot
    for i, rel in enumerate(REL):
        out_ref[AT_COUNTS + i] = count_ref[list_ref[group, place ^ rel]]
    for k in range(CAPS):
        out_ref[AT_RANKING + k] = order_ref[group, k]
    for k in range(4):
        dest = section_of(x * 4 + (y + 4 - k) % 4)
        here = (dest % 4 == y).astype(jnp.int32)
        out_ref[AT_DEST + k] = here * jnp.where(dest // 4 == x, 1, 2)


def make_meta(idx, image_list, patch_count, pref_order, caption_len):
    smem = pl.BlockSpec(memory_space=SMEM)
    return pl.pallas_call(
        meta_kernel,
        out_shape=jax.ShapeDtypeStruct((32,), jnp.int32),
        in_specs=[smem] * 5,
        out_specs=smem,
        name="meta",
    )(idx, image_list, patch_count, pref_order, caption_len)


def pick(which, images):
    chosen = images[-1]
    for k in reversed(range(len(images) - 1)):
        chosen = jnp.where(which == k, images[k], chosen)
    return chosen


def head_columns(head):
    keys = pl.ds(pl.multiple_of(head * HEAD_DIM, HEAD_DIM), HEAD_DIM)
    values = pl.ds(pl.multiple_of((KV_HEADS + head) * HEAD_DIM, HEAD_DIM), HEAD_DIM)
    return keys, values


def with_marks(values, marks):
    values_t = jnp.concatenate(values, axis=0).T
    marks_t = jnp.concatenate(marks, axis=0).T[:16]
    return jnp.concatenate([values_t, marks_t], axis=0).astype(jnp.bfloat16)


def pipelined(count, *stages):
    results = [{} for _ in stages]
    for step in range(count + len(stages) - 1):
        for depth, stage in enumerate(stages):
            g = step - depth
            if 0 <= g < count:
                before = results[depth - 1].pop(g) if depth else None
                results[depth][g] = stage(g, before)
    return [results[-1][g] for g in range(count)]


def column(g):
    return slice(g * HEAD_DIM, (g + 1) * HEAD_DIM)


def own_kernel(q_ref, key_ref, value_ref, acc_ref, max_ref, sum_ref):
    keys = key_ref[...]
    mixed = with_marks(
        [value_ref[...].astype(jnp.float32)], [jnp.ones((CAP_LEN, HEAD_DIM), jnp.float32)]
    )
    diagonal = lax.broadcasted_iota(jnp.int32, (HALF, HALF), 0) <= lax.broadcasted_iota(
        jnp.int32, (HALF, HALF), 1
    )
    minus = jnp.full((HALF, HALF), -jnp.inf, jnp.float32)

    def start(g, _):
        return exact_dot(keys, q_ref[:, column(g)], ((1,), (1,)))

    def soft(g, s):
        s_a = jnp.where(diagonal, s[:HALF, :HALF], minus)
        s_b = s[:HALF, HALF:]
        s_c = jnp.where(diagonal, s[HALF:, HALF:], minus)
        m_low = jnp.max(s_a, axis=0, keepdims=True) * to_base2
        m_high = jnp.max(jnp.maximum(s_b, s_c), axis=0, keepdims=True) * to_base2
        p_a = jnp.exp2(s_a * to_base2 - m_low).astype(jnp.bfloat16)
        p_b = jnp.exp2(s_b * to_base2 - m_high).astype(jnp.bfloat16)
        p_c = jnp.exp2(s_c * to_base2 - m_high).astype(jnp.bfloat16)
        p = jnp.concatenate(
            [
                jnp.concatenate([p_a, p_b], axis=1),
                jnp.concatenate([jnp.zeros_like(p_c), p_c], axis=1),
            ],
            axis=0,
        )
        max_ref[g : g + 1, :] = jnp.concatenate([m_low, m_high], axis=1)
        return p

    def finish(g, p):
        out = exact_dot(mixed, p, ((1,), (0,)))
        acc_ref[column(g), :] = out[:HEAD_DIM]
        sum_ref[g : g + 1, :] = out[HEAD_DIM : HEAD_DIM + 1]

    pipelined(GROUP_HEADS, start, soft, finish)


def image_parts(meta_ref, images, key_cols, value_cols):
    row = lax.broadcasted_iota(jnp.int32, (PATCHES, HEAD_DIM), 0)
    keys, values, marks = [], [], []
    for i, image in enumerate(images):
        live = row < meta_ref[AT_COUNTS + i]
        key = image[:, key_cols].astype(jnp.float32)
        keys.append(jnp.where(live, key, key[0:1, :]).astype(jnp.bfloat16))
        values.append(jnp.where(live, image[:, value_cols].astype(jnp.float32), 0.0))
        marks.append(live.astype(jnp.float32))
    return jnp.concatenate(keys, axis=0), with_marks(values, marks)


def forward_step(head, meta_ref, q_ref, dir_ref, state, images, kept, stat_ref, reward_ref, sum_refs):
    acc_in, max_in, sum_in = state
    p_ref, att_ref, inv_ref = kept
    ss_ref, rd_ref = sum_refs
    keys, mixed = image_parts(meta_ref, images, *head_columns(head))
    dir_t = dir_ref[...].T

    def start(g, _):
        return exact_dot(keys, q_ref[:, column(g)], ((1,), (1,)))

    def attended(p, acc, total):
        out = exact_dot(mixed, p, ((1,), (0,)))
        total = total + out[HEAD_DIM : HEAD_DIM + 1]
        return (acc + out[:HEAD_DIM]) * (1.0 / total), total

    def square_and_reward(att, dir_col):
        ss = jnp.sum((att * att).reshape(16, 8, CAP_LEN), axis=0)
        return ss, jnp.sum((att * dir_col).reshape(16, 8, CAP_LEN), axis=0)

    zero = jnp.zeros((8, CAP_LEN), jnp.float32)
    sums = [zero, zero, jnp.zeros((1, CAP_LEN), jnp.float32)]

    def soft(g, s):
        p = jnp.exp2(s * to_base2 - max_in[g : g + 1, :]).astype(jnp.bfloat16)
        p_ref[g] = p
        return p

    def finish(g, p):
        att, total = attended(p, acc_in[column(g), :], sum_in[g : g + 1, :])
        att_ref[column(g), :] = att
        inv_ref[g : g + 1, :] = 1.0 / total
        ss, rd = square_and_reward(att, dir_t[:, g : g + 1])
        sums[0] += ss
        sums[1] += rd
        sums[2] = jnp.maximum(sums[2], total)

    pipelined(GROUP_HEADS, start, soft, finish)
    inside = jnp.max(sums[2]) < SUM_HIGH

    @pl.when(inside)
    def _():
        ss_ref[...] += sums[0]
        rd_ref[...] += sums[1]

    @pl.when(jnp.logical_not(inside))
    def _():
        for g in range(GROUP_HEADS):
            s = start(g, None)
            old = max_in[g : g + 1, :]
            new = jnp.maximum(old, jnp.max(s, axis=0, keepdims=True) * to_base2)
            shrink = jnp.exp2(old - new)
            p = jnp.exp2(s * to_base2 - new).astype(jnp.bfloat16)
            p_ref[g] = p
            att, total = attended(p, acc_in[column(g), :] * shrink, sum_in[g : g + 1, :] * shrink)
            att_ref[column(g), :] = att
            inv_ref[g : g + 1, :] = 1.0 / total
            ss, rd = square_and_reward(att, dir_t[:, g : g + 1])
            ss_ref[...] += ss
            rd_ref[...] += rd

    @pl.when(head == KV_HEADS - 1)
    def _():
        ss = ss_ref[...]
        rd = rd_ref[...]
        length = meta_ref[AT_LEN]
        inv_rms = lax.rsqrt(jnp.sum(ss, axis=0, keepdims=True) * (1.0 / D) + norm_eps)
        per_token = jnp.sum(rd, axis=0, keepdims=True) * inv_rms
        live = lax.broadcasted_iota(jnp.int32, (1, CAP_LEN), 1) < length
        length_f = jnp.full((1, CAP_LEN), length, jnp.int32).astype(jnp.float32)
        unit = jnp.where(live, 1.0 / length_f, 0.0)
        a = inv_rms * unit
        b = inv_rms * inv_rms * unit * per_token * (1.0 / D)
        stat_ref[...] = jnp.concatenate([a, b, jnp.zeros((6, CAP_LEN), jnp.float32)], axis=0)
        reward = jnp.sum(jnp.where(live, per_token, 0.0), axis=1, keepdims=True)
        reward_ref[...] = jnp.broadcast_to(reward / length_f[:, :1], (8, 128))


ROWS = GROUP_HEADS * HEAD_DIM
Q_SPEC = pl.BlockSpec((CAP_LEN, ROWS), lambda h: (0, h))
ACC_SPEC = pl.BlockSpec((ROWS, CAP_LEN), lambda h: (h, 0))
ROW_SPEC = pl.BlockSpec((GROUP_HEADS, CAP_LEN), lambda h: (h, 0))
SMEM_SPEC = pl.BlockSpec(memory_space=SMEM)
ACC = jax.ShapeDtypeStruct((D, CAP_LEN), jnp.float32)
ROW = jax.ShapeDtypeStruct((COEFS, CAP_LEN), jnp.float32)
TILE = jax.ShapeDtypeStruct((8, 128), jnp.float32)


def by_head(kernel, name, in_specs, out_specs, out_shape, scratch=(), flops=2_000_000_000):
    return pl.pallas_call(
        kernel,
        grid=(KV_HEADS,),
        in_specs=in_specs,
        out_specs=out_specs,
        out_shape=out_shape,
        scratch_shapes=scratch,
        compiler_params=pltpu.CompilerParams(vmem_limit_bytes=BIG_LIMIT),
        cost_estimate=pl.CostEstimate(
            flops=flops, bytes_accessed=16_000_000, transcendentals=4_000_000
        ),
        name=name,
    )


def attend_own(q, own_kv):
    key = pl.BlockSpec((CAP_LEN, HEAD_DIM), lambda h: (0, h))
    value = pl.BlockSpec((CAP_LEN, HEAD_DIM), lambda h: (0, KV_HEADS + h))
    call = by_head(
        own_kernel, "attend_own", [Q_SPEC, key, value], [ACC_SPEC, ROW_SPEC, ROW_SPEC], [ACC, ROW, ROW]
    )
    return call(q, own_kv, own_kv)


def backward_step(head, meta_ref, q_ref, dir_ref, images, kept, stat_ref, outs, coef_ref):
    p_ref, att_ref, inv_ref = kept
    keep_ref, send_ref = outs
    key_cols, value_cols = head_columns(head)
    values = jnp.concatenate([image[:, value_cols] for image in images], axis=0)
    dir_t = dir_ref[...].T
    a = stat_ref[0:1, :]
    b = stat_ref[1:2, :]
    which = lax.broadcasted_iota(jnp.int32, (HEAD_DIM, CAP_LEN), 0)

    key_grad = jnp.zeros((IMG_SLOTS, HEAD_DIM), jnp.float32)
    value_grad = jnp.zeros((IMG_SLOTS, 2 * HEAD_DIM), jnp.float32)

    def prepare(g, _):
        att = att_ref[column(g), :]
        inv = inv_ref[g : g + 1, :]
        factor = a * inv
        rest_grad = -(b * inv) * att
        grad = (factor * dir_t[:, g : g + 1] + rest_grad).astype(jnp.bfloat16)
        delta = jnp.sum(grad.astype(jnp.float32) * att, axis=0, keepdims=True)
        factors = jnp.where(which == head * GROUP_HEADS + g, factor, 0.0)
        return grad, delta, jnp.concatenate([rest_grad, factors], axis=0).astype(jnp.bfloat16)

    def weights(g, before):
        grad, delta, apart = before
        return exact_dot(values, grad, ((1,), (0,))), delta, apart

    def scores(g, before):
        weight_grad, delta, apart = before
        p = p_ref[g]
        score_grad = (p.astype(jnp.float32) * (weight_grad - delta)).astype(jnp.bfloat16)
        return score_grad, apart

    sums = [key_grad, value_grad]

    def add(g, before):
        score_grad, apart = before
        sums[1] += exact_dot(p_ref[g], apart, ((1,), (1,)))
        sums[0] += exact_dot(score_grad, q_ref[:, column(g)], ((1,), (0,)))

    pipelined(GROUP_HEADS, prepare, weights, scores, add)
    key_grad, value_grad = sums
    key_grad = key_grad * scaling
    row = lax.broadcasted_iota(jnp.int32, (PATCHES, HEAD_DIM), 0)
    for i in range(CAPS):
        live = row < meta_ref[AT_COUNTS + i]
        out_ref = keep_ref if i < 4 else send_ref
        part = slice(i * PATCHES, (i + 1) * PATCHES)
        out_ref[i % 4, :, key_cols] = jnp.where(live, key_grad[part], 0.0).astype(jnp.bfloat16)
        out_ref[i % 4, :, value_cols] = jnp.where(
            live, value_grad[part, :HEAD_DIM], 0.0
        ).astype(jnp.bfloat16)
    coef_ref[...] += value_grad[:, HEAD_DIM:]

    @pl.when(head == KV_HEADS - 1)
    def _():
        for i in range(CAPS):
            live = row < meta_ref[AT_COUNTS + i]
            out_ref = keep_ref if i < 4 else send_ref
            coef = coef_ref[i * PATCHES : (i + 1) * PATCHES, :]
            out_ref[i % 4, :, KV_WIDTH:] = in_two(jnp.where(live, coef, 0.0))


def in_two(coef):
    first = coef.astype(jnp.bfloat16).astype(jnp.float32)
    return (first + pltpu.roll(coef - first, COEFS, 1)).astype(jnp.bfloat16)


def from_two(pair):
    pair = pair.astype(jnp.float32)
    lane = lax.broadcasted_iota(jnp.int32, pair.shape, 1)
    return jnp.where(lane < COEFS, pair + pltpu.roll(pair, COEFS, 1), 0.0)


def image_kernel(meta_ref, q_hbm, dir_ref, acc_hbm, max_ref, sum_ref, *rest):
    sources = rest[:CAPS]
    keep_ref, send_ref, reward_ref = rest[CAPS : CAPS + 3]
    q_all, acc_all, image_all, p_all, att_all, inv_all = rest[CAPS + 3 : CAPS + 9]
    stat_ref, ss_ref, rd_ref, coef_ref, q_sem, acc_sem, image_sem = rest[CAPS + 9 :]

    def q_copy(head):
        cols = pl.ds(pl.multiple_of(head * ROWS, ROWS), ROWS)
        return pltpu.make_async_copy(q_hbm.at[:, cols], q_all.at[head], q_sem.at[head])

    def acc_copy(head):
        rows = pl.ds(pl.multiple_of(head * ROWS, ROWS), ROWS)
        return pltpu.make_async_copy(acc_hbm.at[rows, :], acc_all.at[head], acc_sem.at[head])

    copies = [
        pltpu.make_async_copy(source, image_all.at[i], image_sem.at[i])
        for i, source in enumerate(sources)
    ]
    q_copy(0).start()
    for copy in copies:
        copy.start()
    acc_copy(0).start()
    q_copy(1).start()
    acc_copy(1).start()
    ss_ref[...] = jnp.zeros_like(ss_ref)
    rd_ref[...] = jnp.zeros_like(rd_ref)
    coef_ref[...] = jnp.zeros_like(coef_ref)
    for copy in copies:
        copy.wait()
    images = [image_all.at[i] for i in range(CAPS)]

    def of_head(head):
        rows = pl.ds(pl.multiple_of(head * GROUP_HEADS, GROUP_HEADS), GROUP_HEADS)
        kept = (p_all.at[head], att_all.at[head], inv_all.at[head])
        return rows, q_all.at[head], dir_ref.at[rows, :], kept

    @pl.loop(0, KV_HEADS)
    def _(head):
        q_copy(head).wait()
        acc_copy(head).wait()

        @pl.when(head + 2 < KV_HEADS)
        def _():
            q_copy(head + 2).start()
            acc_copy(head + 2).start()

        rows, q_ref, dirs, kept = of_head(head)
        state = (acc_all.at[head], max_ref.at[rows, :], sum_ref.at[rows, :])
        sums = (ss_ref, rd_ref)
        forward_step(head, meta_ref, q_ref, dirs, state, images, kept, stat_ref, reward_ref, sums)

    @pl.loop(0, KV_HEADS)
    def _(head):
        rows, q_ref, dirs, kept = of_head(head)
        outs = (keep_ref, send_ref)
        backward_step(head, meta_ref, q_ref, dirs, images, kept, stat_ref, outs, coef_ref)


def attend_images(meta, q, direction, state, images):
    half = jax.ShapeDtypeStruct((4, PATCHES, WIDE), jnp.bfloat16)
    any_space = pl.BlockSpec(memory_space=pl.ANY)
    vmem = pl.BlockSpec(memory_space=VMEM)
    row = VMEM((8, CAP_LEN), jnp.float32)
    call = pl.pallas_call(
        image_kernel,
        in_specs=[SMEM_SPEC, any_space, vmem, any_space, vmem, vmem] + [any_space] * CAPS,
        out_specs=[vmem] * 3,
        out_shape=[half, half, TILE],
        scratch_shapes=[
            VMEM((KV_HEADS, CAP_LEN, ROWS), jnp.bfloat16),
            VMEM((KV_HEADS, ROWS, CAP_LEN), jnp.float32),
            VMEM((CAPS, PATCHES, KV_WIDTH), jnp.bfloat16),
            VMEM((KV_HEADS, GROUP_HEADS, IMG_SLOTS, CAP_LEN), jnp.bfloat16),
            VMEM((KV_HEADS, ROWS, CAP_LEN), jnp.float32),
            VMEM((KV_HEADS, GROUP_HEADS, CAP_LEN), jnp.float32),
            row,
            row,
            row,
            VMEM((IMG_SLOTS, HEAD_DIM), jnp.float32),
            pltpu.SemaphoreType.DMA((KV_HEADS,)),
            pltpu.SemaphoreType.DMA((KV_HEADS,)),
            pltpu.SemaphoreType.DMA((CAPS,)),
        ],
        compiler_params=pltpu.CompilerParams(vmem_limit_bytes=BIG_LIMIT),
        cost_estimate=pl.CostEstimate(
            flops=8_000_000_000, bytes_accessed=18_000_000, transcendentals=6_000_000
        ),
        name="attend_images",
    )
    return call(meta, q, direction, *state, *images)


def group_loss(place, rewards, meta_ref):
    lane = lax.broadcasted_iota(jnp.int32, (8, 128), 1)
    sub = lax.broadcasted_iota(jnp.int32, (8, 128), 0)
    by_lane = jnp.zeros((8, 128), jnp.float32)
    by_sub = jnp.zeros((8, 128), jnp.float32)
    for rel in range(CAPS):
        tile = rewards[rel // 2][...]
        value = jnp.where((place ^ rel) % 2 == 0, tile[0:1, :], tile[1:2, :])
        by_lane = jnp.where(lane == (place ^ rel), value, by_lane)
        by_sub = jnp.where(sub == (place ^ rel), value, by_sub)
    rank_lane = jnp.full((8, 128), CAPS, jnp.int32)
    rank_sub = jnp.zeros((8, 128), jnp.int32)
    for k in range(CAPS):
        who = meta_ref[AT_RANKING + k]
        rank_lane = jnp.where(lane == who, k, rank_lane)
        rank_sub = jnp.where(sub == who, k, rank_sub)
    real = lane < CAPS
    better = real & (rank_sub < rank_lane)
    worse = real & (rank_sub > rank_lane)
    margin = by_lane - by_sub
    soft = jnp.maximum(margin, 0.0) + jnp.log1p(jnp.exp(-jnp.abs(margin)))
    pairs = jnp.where(better, soft, 0.0)
    loss = jnp.sum(jnp.sum(pairs, axis=0, keepdims=True), axis=1, keepdims=True)
    up = 1.0 / (1.0 + jnp.exp(margin))
    down = 1.0 / (1.0 + jnp.exp(-margin))
    grads = jnp.where(worse, up, 0.0) - jnp.where(better, down, 0.0)
    grads = jnp.sum(grads, axis=1, keepdims=True) * loss_scale
    sub_col = sub[:, :1]
    mine = jnp.sum(jnp.where(sub_col == place, grads, 0.0), axis=0, keepdims=True)
    other = jnp.sum(jnp.where(sub_col == (place ^ 1), grads, 0.0), axis=0, keepdims=True)
    return loss, mine, other


def scaled_sum_kernel(meta_ref, keep_ref, recv_ref, *rest):
    rewards = rest[:4]
    *outs, loss_ref = rest[4:]
    loss, mine, other = group_loss(meta_ref[AT_PLACE], rewards, meta_ref)
    loss_ref[...] = jnp.broadcast_to(loss, (8, 128))
    for i, out_ref in enumerate(outs):
        kept, sent = keep_ref[i], recv_ref[i]
        total = kept[:, :KV_WIDTH].astype(jnp.float32) * mine
        total = total + sent[:, :KV_WIDTH].astype(jnp.float32) * other
        coef = from_two(kept[:, KV_WIDTH:]) * mine + from_two(sent[:, KV_WIDTH:]) * other
        out_ref[:, :KV_WIDTH] = total.astype(out_ref.dtype)
        wide = out_ref.dtype == jnp.float32
        out_ref[:, KV_WIDTH:] = coef if wide else in_two(coef)


def in_vmem(kernel, name, count, out_shape, meta=True):
    vmem = pl.BlockSpec(memory_space=VMEM)
    return pl.pallas_call(
        kernel,
        in_specs=[SMEM_SPEC] * meta + [vmem] * count,
        out_specs=[vmem] * len(out_shape),
        out_shape=out_shape,
        compiler_params=pltpu.CompilerParams(vmem_limit_bytes=VMEM_LIMIT),
        name=name,
    )


WIRE = jax.ShapeDtypeStruct((PATCHES, WIDE), jnp.bfloat16)
TOTAL = jax.ShapeDtypeStruct((PATCHES, WIDE), jnp.float32)


def scaled_sum(meta, keep, recv, rewards):
    outs = [TOTAL, WIRE, WIRE, WIRE, TILE]
    call = in_vmem(scaled_sum_kernel, "scaled_sum", 6, outs)
    return call(meta, keep, recv, *rewards)


def in_three(value):
    terms = []
    for _ in range(3):
        term = value.astype(jnp.bfloat16).astype(jnp.float32)
        terms.append(term)
        value = value - term
    return terms


def store_loss(ref, loss):
    lane = lax.broadcasted_iota(jnp.int32, (PATCHES, 128), 1)
    first, second, third = (term[:1] for term in in_three(loss))
    row = jnp.where(lane == 0, first, jnp.where(lane == 1, second, third))
    ref[:, KV_WIDTH:] = row.astype(jnp.bfloat16)


def read_loss(ref):
    row = ref[:8, KV_WIDTH:].astype(jnp.float32)
    return jnp.broadcast_to(row[:, 0:1] + row[:, 1:2] + row[:, 2:3], (8, 128))


def sum_kernel(own_ref, a_ref, b_ref, c_ref, dir_ref, l0_ref, l1_ref, out_ref):
    own = own_ref[...]
    total, coef = own[:, :KV_WIDTH], own[:, KV_WIDTH:]
    for part in (a_ref, b_ref, c_ref):
        total = total + part[:, :KV_WIDTH].astype(jnp.float32)
        coef = coef + from_two(part[:, KV_WIDTH:])
    out_ref[:, : KV_WIDTH // 2] = total[:, : KV_WIDTH // 2].astype(out_ref.dtype)
    for head in range(KV_HEADS):
        cols = column(KV_HEADS + head)
        value = total[:, cols]
        for j in range(head * GROUP_HEADS, (head + 1) * GROUP_HEADS):
            value = value + coef[:, j : j + 1] * dir_ref[j : j + 1, :]
        out_ref[:, cols] = value.astype(out_ref.dtype)
    store_loss(out_ref, l0_ref[...] + l1_ref[...])


def group_sum(own, parts, direction, losses):
    call = in_vmem(sum_kernel, "group_sum", 7, [WIRE], meta=False)
    return call(own, *parts, direction, *losses)[0]


def sort_kernel(meta_ref, s0, s1, s2, s3, keep_ref, send_ref, loss_ref):
    total = jnp.zeros((PATCHES, KV_WIDTH), jnp.float32)
    kept = jnp.zeros((PATCHES, KV_WIDTH), jnp.float32)
    for k, part in enumerate((s0, s1, s2, s3)):
        dest = meta_ref[AT_DEST + k]
        value = part[:, :KV_WIDTH].astype(jnp.float32)
        kept = kept + jnp.where(dest == 1, value, 0.0)
        total = total + jnp.where(dest == 2, value, 0.0)
    keep_ref[...] = kept
    send_ref[:, :KV_WIDTH] = total.astype(send_ref.dtype)
    loss = (read_loss(s0) + read_loss(s2)) + (read_loss(s1) + read_loss(s3))
    store_loss(send_ref, loss)
    loss_ref[...] = loss


def sort_by_owner(meta, parts):
    grad = jax.ShapeDtypeStruct((PATCHES, KV_WIDTH), jnp.float32)
    return in_vmem(sort_kernel, "sort_by_owner", 4, [grad, WIRE, TILE])(meta, *parts)


def last_kernel(keep_ref, recv_ref, loss_in_ref, out_ref, loss_ref):
    out_ref[0] = keep_ref[...] + recv_ref[:, :KV_WIDTH].astype(jnp.float32)
    loss_ref[...] = loss_in_ref[...] + read_loss(recv_ref)


def last_sum(kept, recv, loss):
    grad = jax.ShapeDtypeStruct((1, PATCHES, KV_WIDTH), jnp.float32)
    return in_vmem(last_kernel, "last_sum", 3, [grad, TILE], meta=False)(kept, recv, loss)


def along_y(value, step):
    pairs = [(s, s // 4 * 4 + (s + step) % 4) for s in range(8)]
    return lax.ppermute(value, "segment", pairs)


def across(value, axis, mask):
    size = lax.axis_size(axis)
    return lax.ppermute(value, axis, [(i, i ^ mask) for i in range(size)])


def per_device(
    queries, caption_kv, caption_len, image_kv, patch_count, image_list, pref_order, reward_dir
):
    idx = jnp.stack([lax.axis_index("segment"), lax.axis_index("tp")]).astype(jnp.int32)
    image = image_kv[0]
    q = queries[0]
    direction = reward_dir.reshape(KV_HEADS * GROUP_HEADS, HEAD_DIM)
    meta = make_meta(idx, image_list, patch_count, pref_order, caption_len)

    seen = [image] + [along_y(image, step) for step in (1, 2, 3)]
    wanted = pick(meta[AT_FOR_PARTNER], seen)
    own = pick(meta[AT_OWN], [*seen, across(wanted, "segment", 4)])
    acc, top, total = attend_own(q, caption_kv[0])
    others = [across(own, "tp", mask) for mask in (2, 4, 6)]
    *others, top = lax.optimization_barrier((*others, top))
    same_core = [own, *others]
    images = same_core + [across(one, "tp", 1) for one in same_core]

    keep, send, reward = attend_images(meta, q, direction, (acc, top, total), images)
    recv = across(send, "tp", 1)
    other = across(reward, "tp", 1)
    second = lax.axis_index("tp") % 2 == 1
    row = lax.broadcasted_iota(jnp.int32, reward.shape, 0)
    pair = jnp.where((row == 1) == second, reward, other)
    rewards = [pair] + [across(pair, "tp", mask) for mask in (2, 4, 6)]
    mine, to_z1, to_z2, to_z3, loss = scaled_sum(meta, keep, recv, rewards)
    parts = [across(to_z1, "tp", 2), across(to_z2, "tp", 4), across(to_z3, "tp", 6)]
    loss = loss + across(loss, "tp", 16)
    losses = (loss, across(loss, "tp", 8))
    total = group_sum(mine, parts, direction, losses)
    totals = [total] + [along_y(total, step) for step in (1, 2, 3)]
    kept, away, loss = sort_by_owner(meta, totals)
    image_grad, loss = last_sum(kept, across(away, "segment", 4), loss)
    return (loss[0, 0], reward[0, :1], image_grad)


def solution(mesh):
    placed = (
        P(("segment", "tp"), None, None),
        P(("segment", "tp"), None, None),
        P(("segment", "tp")),
        P(("segment", "tp"), None, None),
        P(),
        P(),
        P(),
        P(),
    )
    return jax.shard_map(
        per_device,
        mesh=mesh,
        in_specs=placed,
        out_specs=(P(), P(("segment", "tp")), P(("segment", "tp"), None, None)),
        check_vma=False,
    )
```

```python
import functools
import math

import jax
import jax.numpy as jnp
from jax import lax
from jax.experimental import pallas as pl
from jax.experimental.pallas import tpu as pltpu
from jax.sharding import PartitionSpec as P

D = 8192
KV_HEADS = 8
HEAD_DIM = 128
CAP_LEN = 256
PATCHES = 48
CAPS = 8
GROUP_HEADS = 8
KV_WIDTH = 2048
COLUMNS = 32
IMG_SLOTS = CAPS * PATCHES
COEFS = KV_HEADS * GROUP_HEADS
WIDE = KV_WIDTH + 2 * COEFS
HALF = CAP_LEN // 2

norm_eps = 1e-06
loss_scale = 65536.0
scaling = 1.0 / math.sqrt(HEAD_DIM)
to_base2 = scaling * math.log2(math.e)

SMEM = pltpu.SMEM
VMEM = pltpu.VMEM
VMEM_LIMIT = 16 * 1024 * 1024
BIG_LIMIT = 48 * 1024 * 1024

AT_FOR_PARTNER, AT_OWN, AT_PLACE, AT_LEN = 0, 1, 2, 3
AT_COUNTS, AT_RANKING, AT_DEST = 8, 16, 24

REL = (0, 2, 4, 6, 1, 3, 5, 7)

SUM_HIGH = 2.0**60


def exact_dot(a, b, dims):
    return lax.dot_general(a, b, (dims, ((), ())), preferred_element_type=jnp.float32)


def meta_kernel(idx_ref, list_ref, count_ref, order_ref, len_ref, out_ref):
    seg = idx_ref[0]
    col = idx_ref[1]
    x = seg // 4
    y = seg % 4
    slot = col // CAPS
    place = col % CAPS

    def section_of(section):
        return list_ref[section * 4 + slot, place] // COLUMNS

    own = section_of(seg)
    partner = section_of((1 - x) * 4 + y)
    out_ref[AT_FOR_PARTNER] = (y + 4 - partner % 4) % 4
    out_ref[AT_OWN] = jnp.where(own // 4 == x, (y + 4 - own % 4) % 4, 4)
    out_ref[AT_PLACE] = place
    out_ref[AT_LEN] = len_ref[0]
    group = seg * 4 + slot
    for i, rel in enumerate(REL):
        out_ref[AT_COUNTS + i] = count_ref[list_ref[group, place ^ rel]]
    for k in range(CAPS):
        out_ref[AT_RANKING + k] = order_ref[group, k]
    for k in range(4):
        dest = section_of(x * 4 + (y + 4 - k) % 4)
        here = (dest % 4 == y).astype(jnp.int32)
        out_ref[AT_DEST + k] = here * jnp.where(dest // 4 == x, 1, 2)


def make_meta(idx, image_list, patch_count, pref_order, caption_len):
    smem = pl.BlockSpec(memory_space=SMEM)
    return pl.pallas_call(
        meta_kernel,
        out_shape=jax.ShapeDtypeStruct((32,), jnp.int32),
        in_specs=[smem] * 5,
        out_specs=smem,
        name="meta",
    )(idx, image_list, patch_count, pref_order, caption_len)


def pick(which, images):
    chosen = images[-1]
    for k in reversed(range(len(images) - 1)):
        chosen = jnp.where(which == k, images[k], chosen)
    return chosen


def head_columns(head):
    keys = pl.ds(pl.multiple_of(head * HEAD_DIM, HEAD_DIM), HEAD_DIM)
    values = pl.ds(pl.multiple_of((KV_HEADS + head) * HEAD_DIM, HEAD_DIM), HEAD_DIM)
    return keys, values


def with_marks(values, marks):
    values_t = jnp.concatenate(values, axis=0).T
    marks_t = jnp.concatenate(marks, axis=0).T[:16]
    return jnp.concatenate([values_t, marks_t], axis=0).astype(jnp.bfloat16)


def pipelined(count, *stages):
    results = [{} for _ in stages]
    for step in range(count + len(stages) - 1):
        for depth, stage in enumerate(stages):
            g = step - depth
            if 0 <= g < count:
                before = results[depth - 1].pop(g) if depth else None
                results[depth][g] = stage(g, before)
    return [results[-1][g] for g in range(count)]


def column(g):
    return slice(g * HEAD_DIM, (g + 1) * HEAD_DIM)


def own_kernel(q_ref, key_ref, value_ref, acc_ref, max_ref, sum_ref):
    keys = key_ref[...]
    mixed = with_marks(
        [value_ref[...].astype(jnp.float32)], [jnp.ones((CAP_LEN, HEAD_DIM), jnp.float32)]
    )
    diagonal = lax.broadcasted_iota(jnp.int32, (HALF, HALF), 0) <= lax.broadcasted_iota(
        jnp.int32, (HALF, HALF), 1
    )
    minus = jnp.full((HALF, HALF), -jnp.inf, jnp.float32)

    def start(g, _):
        return exact_dot(keys, q_ref[:, column(g)], ((1,), (1,)))

    def soft(g, s):
        s_a = jnp.where(diagonal, s[:HALF, :HALF], minus)
        s_b = s[:HALF, HALF:]
        s_c = jnp.where(diagonal, s[HALF:, HALF:], minus)
        m_low = jnp.max(s_a, axis=0, keepdims=True) * to_base2
        m_high = jnp.max(jnp.maximum(s_b, s_c), axis=0, keepdims=True) * to_base2
        p_a = jnp.exp2(s_a * to_base2 - m_low).astype(jnp.bfloat16)
        p_b = jnp.exp2(s_b * to_base2 - m_high).astype(jnp.bfloat16)
        p_c = jnp.exp2(s_c * to_base2 - m_high).astype(jnp.bfloat16)
        p = jnp.concatenate(
            [
                jnp.concatenate([p_a, p_b], axis=1),
                jnp.concatenate([jnp.zeros_like(p_c), p_c], axis=1),
            ],
            axis=0,
        )
        max_ref[g : g + 1, :] = jnp.concatenate([m_low, m_high], axis=1)
        return p

    def finish(g, p):
        out = exact_dot(mixed, p, ((1,), (0,)))
        acc_ref[column(g), :] = out[:HEAD_DIM]
        sum_ref[g : g + 1, :] = out[HEAD_DIM : HEAD_DIM + 1]

    pipelined(GROUP_HEADS, start, soft, finish)


def image_parts(meta_ref, images, key_cols, value_cols):
    row = lax.broadcasted_iota(jnp.int32, (PATCHES, HEAD_DIM), 0)
    keys, values, marks = [], [], []
    for i, image in enumerate(images):
        live = row < meta_ref[AT_COUNTS + i]
        key = image[:, key_cols].astype(jnp.float32)
        keys.append(jnp.where(live, key, key[0:1, :]).astype(jnp.bfloat16))
        values.append(jnp.where(live, image[:, value_cols].astype(jnp.float32), 0.0))
        marks.append(live.astype(jnp.float32))
    return jnp.concatenate(keys, axis=0), with_marks(values, marks)


def forward_step(head, exact, meta_ref, q_ref, dir_ref, state, images, kept, sum_refs):
    acc_in, max_in, sum_in = state
    p_ref, att_ref, inv_ref = kept
    ss_ref, rd_ref, top_ref = sum_refs
    keys, mixed = image_parts(meta_ref, images, *head_columns(head))
    dir_t = dir_ref[...].T
    sums = [ss_ref[...], rd_ref[...], top_ref[...]]

    def start(g, _):
        return exact_dot(keys, q_ref[:, column(g)], ((1,), (1,)))

    def soft(g, s):
        old = max_in[g : g + 1, :]
        shrink = None
        if exact:
            new = jnp.maximum(old, jnp.max(s, axis=0, keepdims=True) * to_base2)
            shrink, old = jnp.exp2(old - new), new
        p = jnp.exp2(s * to_base2 - old).astype(jnp.bfloat16)
        p_ref[g] = p
        return p, shrink

    def finish(g, before):
        p, shrink = before
        acc, total = acc_in[column(g), :], sum_in[g : g + 1, :]
        if exact:
            acc, total = acc * shrink, total * shrink
        out = exact_dot(mixed, p, ((1,), (0,)))
        total = total + out[HEAD_DIM : HEAD_DIM + 1]
        inv = 1.0 / total
        att = (acc + out[:HEAD_DIM]) * inv
        att_ref[column(g), :] = att
        inv_ref[g : g + 1, :] = inv
        sums[0] += jnp.sum((att * att).reshape(16, 8, CAP_LEN), axis=0)
        sums[1] += jnp.sum((att * dir_t[:, g : g + 1]).reshape(16, 8, CAP_LEN), axis=0)
        sums[2] = jnp.maximum(sums[2], total)

    pipelined(GROUP_HEADS, start, soft, finish)
    ss_ref[...], rd_ref[...], top_ref[...] = sums


def token_factors(meta_ref, ss_ref, rd_ref, stat_ref, reward_ref):
    length = meta_ref[AT_LEN]
    inv_rms = lax.rsqrt(jnp.sum(ss_ref[...], axis=0, keepdims=True) * (1.0 / D) + norm_eps)
    per_token = jnp.sum(rd_ref[...], axis=0, keepdims=True) * inv_rms
    live = lax.broadcasted_iota(jnp.int32, (1, CAP_LEN), 1) < length
    length_f = jnp.full((1, CAP_LEN), length, jnp.int32).astype(jnp.float32)
    unit = jnp.where(live, 1.0 / length_f, 0.0)
    a = inv_rms * unit
    b = inv_rms * inv_rms * unit * per_token * (1.0 / D)
    stat_ref[...] = jnp.concatenate([a, b, jnp.zeros((6, CAP_LEN), jnp.float32)], axis=0)
    reward = jnp.sum(jnp.where(live, per_token, 0.0), axis=1, keepdims=True)
    reward_ref[...] = jnp.broadcast_to(reward / length_f[:, :1], (8, 128))


ROWS = GROUP_HEADS * HEAD_DIM
Q_SPEC = pl.BlockSpec((CAP_LEN, ROWS), lambda h: (0, h))
ACC_SPEC = pl.BlockSpec((ROWS, CAP_LEN), lambda h: (h, 0))
ROW_SPEC = pl.BlockSpec((GROUP_HEADS, CAP_LEN), lambda h: (h, 0))
SMEM_SPEC = pl.BlockSpec(memory_space=SMEM)
ACC = jax.ShapeDtypeStruct((D, CAP_LEN), jnp.float32)
ROW = jax.ShapeDtypeStruct((COEFS, CAP_LEN), jnp.float32)
TILE = jax.ShapeDtypeStruct((8, 128), jnp.float32)


def by_head(kernel, name, in_specs, out_specs, out_shape, scratch=(), flops=2_000_000_000):
    return pl.pallas_call(
        kernel,
        grid=(KV_HEADS,),
        in_specs=in_specs,
        out_specs=out_specs,
        out_shape=out_shape,
        scratch_shapes=scratch,
        compiler_params=pltpu.CompilerParams(vmem_limit_bytes=VMEM_LIMIT),
        cost_estimate=pl.CostEstimate(
            flops=flops, bytes_accessed=16_000_000, transcendentals=4_000_000
        ),
        name=name,
    )


def attend_own(q, own_kv):
    key = pl.BlockSpec((CAP_LEN, HEAD_DIM), lambda h: (0, h))
    value = pl.BlockSpec((CAP_LEN, HEAD_DIM), lambda h: (0, KV_HEADS + h))
    call = by_head(
        own_kernel, "attend_own", [Q_SPEC, key, value], [ACC_SPEC, ROW_SPEC, ROW_SPEC], [ACC, ROW, ROW]
    )
    return call(q, own_kv, own_kv)


def backward_step(head, meta_ref, q_ref, dir_ref, images, kept, stat_ref, outs, coef_ref):
    p_ref, att_ref, inv_ref = kept
    keep_ref, send_ref = outs
    key_cols, value_cols = head_columns(head)
    values = jnp.concatenate([image[:, value_cols] for image in images], axis=0)
    dir_t = dir_ref[...].T
    a = stat_ref[0:1, :]
    b = stat_ref[1:2, :]
    which = lax.broadcasted_iota(jnp.int32, (HEAD_DIM, CAP_LEN), 0)

    key_grad = jnp.zeros((IMG_SLOTS, HEAD_DIM), jnp.float32)
    value_grad = jnp.zeros((IMG_SLOTS, 2 * HEAD_DIM), jnp.float32)

    def prepare(g, _):
        att = att_ref[column(g), :]
        inv = inv_ref[g : g + 1, :]
        factor = a * inv
        rest_grad = -(b * inv) * att
        grad = (factor * dir_t[:, g : g + 1] + rest_grad).astype(jnp.bfloat16)
        delta = jnp.sum(grad.astype(jnp.float32) * att, axis=0, keepdims=True)
        factors = jnp.where(which == head * GROUP_HEADS + g, factor, 0.0)
        return grad, delta, jnp.concatenate([rest_grad, factors], axis=0).astype(jnp.bfloat16)

    def weights(g, before):
        grad, delta, apart = before
        return exact_dot(values, grad, ((1,), (0,))), delta, apart

    def scores(g, before):
        weight_grad, delta, apart = before
        p = p_ref[g]
        score_grad = (p.astype(jnp.float32) * (weight_grad - delta)).astype(jnp.bfloat16)
        return score_grad, apart

    sums = [key_grad, value_grad]

    def add(g, before):
        score_grad, apart = before
        sums[1] += exact_dot(p_ref[g], apart, ((1,), (1,)))
        sums[0] += exact_dot(score_grad, q_ref[:, column(g)], ((1,), (0,)))

    pipelined(GROUP_HEADS, prepare, weights, scores, add)
    key_grad, value_grad = sums
    key_grad = key_grad * scaling
    row = lax.broadcasted_iota(jnp.int32, (PATCHES, HEAD_DIM), 0)
    for i in range(CAPS):
        live = row < meta_ref[AT_COUNTS + i]
        out_ref = keep_ref if i < 4 else send_ref
        part = slice(i * PATCHES, (i + 1) * PATCHES)
        out_ref[i % 4, :, key_cols] = jnp.where(live, key_grad[part], 0.0).astype(jnp.bfloat16)
        out_ref[i % 4, :, value_cols] = jnp.where(
            live, value_grad[part, :HEAD_DIM], 0.0
        ).astype(jnp.bfloat16)
    coef_ref[...] += value_grad[:, HEAD_DIM:]

    @pl.when(head == KV_HEADS - 1)
    def _():
        for i in range(CAPS):
            live = row < meta_ref[AT_COUNTS + i]
            out_ref = keep_ref if i < 4 else send_ref
            coef = coef_ref[i * PATCHES : (i + 1) * PATCHES, :]
            out_ref[i % 4, :, KV_WIDTH:] = in_two(jnp.where(live, coef, 0.0))


def in_two(coef):
    first = coef.astype(jnp.bfloat16).astype(jnp.float32)
    return (first + pltpu.roll(coef - first, COEFS, 1)).astype(jnp.bfloat16)


def from_two(pair):
    pair = pair.astype(jnp.float32)
    lane = lax.broadcasted_iota(jnp.int32, pair.shape, 1)
    return jnp.where(lane < COEFS, pair + pltpu.roll(pair, COEFS, 1), 0.0)


def image_kernel(meta_ref, q_hbm, dir_ref, acc_hbm, max_ref, sum_ref, *rest):
    sources = rest[:CAPS]
    keep_ref, send_ref, reward_ref = rest[CAPS : CAPS + 3]
    q_all, acc_all, image_all, p_all, att_all, inv_all = rest[CAPS + 3 : CAPS + 9]
    stat_ref, ss_ref, rd_ref, top_ref, coef_ref, q_sem, acc_sem, image_sem = rest[CAPS + 9 :]

    def q_copy(head):
        cols = pl.ds(pl.multiple_of(head * ROWS, ROWS), ROWS)
        return pltpu.make_async_copy(q_hbm.at[:, cols], q_all.at[head], q_sem.at[head])

    def acc_copy(head):
        rows = pl.ds(pl.multiple_of(head * ROWS, ROWS), ROWS)
        return pltpu.make_async_copy(acc_hbm.at[rows, :], acc_all.at[head], acc_sem.at[head])

    copies = [
        pltpu.make_async_copy(source, image_all.at[i], image_sem.at[i])
        for i, source in enumerate(sources)
    ]
    q_copy(0).start()
    for copy in copies:
        copy.start()
    acc_copy(0).start()
    q_copy(1).start()
    acc_copy(1).start()
    sums = (ss_ref, rd_ref, top_ref)
    for ref in (*sums, coef_ref):
        ref[...] = jnp.zeros_like(ref)
    for copy in copies:
        copy.wait()
    images = [image_all.at[i] for i in range(CAPS)]

    def of_head(head):
        rows = pl.ds(pl.multiple_of(head * GROUP_HEADS, GROUP_HEADS), GROUP_HEADS)
        kept = (p_all.at[head], att_all.at[head], inv_all.at[head])
        return rows, q_all.at[head], dir_ref.at[rows, :], kept

    def forward_head(head, exact):
        rows, q_ref, dirs, kept = of_head(head)
        state = (acc_all.at[head], max_ref.at[rows, :], sum_ref.at[rows, :])
        forward_step(head, exact, meta_ref, q_ref, dirs, state, images, kept, sums)

    @pl.loop(0, KV_HEADS)
    def _(head):
        q_copy(head).wait()
        acc_copy(head).wait()

        @pl.when(head + 2 < KV_HEADS)
        def _():
            q_copy(head + 2).start()
            acc_copy(head + 2).start()

        forward_head(head, False)

    @pl.when(jnp.logical_not(jnp.max(top_ref[...]) < SUM_HIGH))
    def _():
        for ref in sums:
            ref[...] = jnp.zeros_like(ref)

        @pl.loop(0, KV_HEADS)
        def _(head):
            forward_head(head, True)

    token_factors(meta_ref, ss_ref, rd_ref, stat_ref, reward_ref)

    @pl.loop(0, KV_HEADS)
    def _(head):
        rows, q_ref, dirs, kept = of_head(head)
        outs = (keep_ref, send_ref)
        backward_step(head, meta_ref, q_ref, dirs, images, kept, stat_ref, outs, coef_ref)


def attend_images(meta, q, direction, state, images):
    half = jax.ShapeDtypeStruct((4, PATCHES, WIDE), jnp.bfloat16)
    any_space = pl.BlockSpec(memory_space=pl.ANY)
    vmem = pl.BlockSpec(memory_space=VMEM)
    row = VMEM((8, CAP_LEN), jnp.float32)
    call = pl.pallas_call(
        image_kernel,
        in_specs=[SMEM_SPEC, any_space, vmem, any_space, vmem, vmem] + [any_space] * CAPS,
        out_specs=[vmem] * 3,
        out_shape=[half, half, TILE],
        scratch_shapes=[
            VMEM((KV_HEADS, CAP_LEN, ROWS), jnp.bfloat16),
            VMEM((KV_HEADS, ROWS, CAP_LEN), jnp.float32),
            VMEM((CAPS, PATCHES, KV_WIDTH), jnp.bfloat16),
            VMEM((KV_HEADS, GROUP_HEADS, IMG_SLOTS, CAP_LEN), jnp.bfloat16),
            VMEM((KV_HEADS, ROWS, CAP_LEN), jnp.float32),
            VMEM((KV_HEADS, GROUP_HEADS, CAP_LEN), jnp.float32),
            row,
            row,
            row,
            VMEM((1, CAP_LEN), jnp.float32),
            VMEM((IMG_SLOTS, HEAD_DIM), jnp.float32),
            pltpu.SemaphoreType.DMA((KV_HEADS,)),
            pltpu.SemaphoreType.DMA((KV_HEADS,)),
            pltpu.SemaphoreType.DMA((CAPS,)),
        ],
        compiler_params=pltpu.CompilerParams(vmem_limit_bytes=BIG_LIMIT),
        cost_estimate=pl.CostEstimate(
            flops=8_000_000_000, bytes_accessed=18_000_000, transcendentals=6_000_000
        ),
        name="attend_images",
    )
    return call(meta, q, direction, *state, *images)


def group_loss(place, rewards, meta_ref):
    lane = lax.broadcasted_iota(jnp.int32, (8, 128), 1)
    sub = lax.broadcasted_iota(jnp.int32, (8, 128), 0)
    by_lane = jnp.zeros((8, 128), jnp.float32)
    by_sub = jnp.zeros((8, 128), jnp.float32)
    for rel in range(CAPS):
        tile = rewards[rel // 2][...]
        value = jnp.where((place ^ rel) % 2 == 0, tile[0:1, :], tile[1:2, :])
        by_lane = jnp.where(lane == (place ^ rel), value, by_lane)
        by_sub = jnp.where(sub == (place ^ rel), value, by_sub)
    rank_lane = jnp.full((8, 128), CAPS, jnp.int32)
    rank_sub = jnp.zeros((8, 128), jnp.int32)
    for k in range(CAPS):
        who = meta_ref[AT_RANKING + k]
        rank_lane = jnp.where(lane == who, k, rank_lane)
        rank_sub = jnp.where(sub == who, k, rank_sub)
    real = lane < CAPS
    better = real & (rank_sub < rank_lane)
    worse = real & (rank_sub > rank_lane)
    margin = by_lane - by_sub
    soft = jnp.maximum(margin, 0.0) + jnp.log1p(jnp.exp(-jnp.abs(margin)))
    pairs = jnp.where(better, soft, 0.0)
    loss = jnp.sum(jnp.sum(pairs, axis=0, keepdims=True), axis=1, keepdims=True)
    up = 1.0 / (1.0 + jnp.exp(margin))
    down = 1.0 / (1.0 + jnp.exp(-margin))
    grads = jnp.where(worse, up, 0.0) - jnp.where(better, down, 0.0)
    grads = jnp.sum(grads, axis=1, keepdims=True) * loss_scale
    sub_col = sub[:, :1]
    mine = jnp.sum(jnp.where(sub_col == place, grads, 0.0), axis=0, keepdims=True)
    other = jnp.sum(jnp.where(sub_col == (place ^ 1), grads, 0.0), axis=0, keepdims=True)
    return loss, mine, other


def scaled_sum_kernel(meta_ref, keep_ref, recv_ref, *rest):
    rewards = rest[:4]
    *outs, loss_ref = rest[4:]
    loss, mine, other = group_loss(meta_ref[AT_PLACE], rewards, meta_ref)
    loss_ref[...] = jnp.broadcast_to(loss, (8, 128))
    for i, out_ref in enumerate(outs):
        kept, sent = keep_ref[i], recv_ref[i]
        total = kept[:, :KV_WIDTH].astype(jnp.float32) * mine
        total = total + sent[:, :KV_WIDTH].astype(jnp.float32) * other
        coef = from_two(kept[:, KV_WIDTH:]) * mine + from_two(sent[:, KV_WIDTH:]) * other
        out_ref[:, :KV_WIDTH] = total.astype(out_ref.dtype)
        wide = out_ref.dtype == jnp.float32
        out_ref[:, KV_WIDTH:] = coef if wide else in_two(coef)


def in_vmem(kernel, name, count, out_shape, meta=True):
    vmem = pl.BlockSpec(memory_space=VMEM)
    return pl.pallas_call(
        kernel,
        in_specs=[SMEM_SPEC] * meta + [vmem] * count,
        out_specs=[vmem] * len(out_shape),
        out_shape=out_shape,
        compiler_params=pltpu.CompilerParams(vmem_limit_bytes=VMEM_LIMIT),
        name=name,
    )


WIRE = jax.ShapeDtypeStruct((PATCHES, WIDE), jnp.bfloat16)
TOTAL = jax.ShapeDtypeStruct((PATCHES, WIDE), jnp.float32)


def scaled_sum(meta, keep, recv, rewards):
    outs = [TOTAL, WIRE, WIRE, WIRE, TILE]
    call = in_vmem(scaled_sum_kernel, "scaled_sum", 6, outs)
    return call(meta, keep, recv, *rewards)


def in_three(value):
    terms = []
    for _ in range(3):
        term = value.astype(jnp.bfloat16).astype(jnp.float32)
        terms.append(term)
        value = value - term
    return terms


def store_loss(ref, loss):
    lane = lax.broadcasted_iota(jnp.int32, (PATCHES, 128), 1)
    first, second, third = (term[:1] for term in in_three(loss))
    row = jnp.where(lane == 0, first, jnp.where(lane == 1, second, third))
    ref[:, KV_WIDTH:] = row.astype(jnp.bfloat16)


def read_loss(ref):
    row = ref[:8, KV_WIDTH:].astype(jnp.float32)
    return jnp.broadcast_to(row[:, 0:1] + row[:, 1:2] + row[:, 2:3], (8, 128))


def sum_kernel(own_ref, a_ref, b_ref, c_ref, dir_ref, l0_ref, l1_ref, out_ref):
    own = own_ref[...]
    total, coef = own[:, :KV_WIDTH], own[:, KV_WIDTH:]
    for part in (a_ref, b_ref, c_ref):
        total = total + part[:, :KV_WIDTH].astype(jnp.float32)
        coef = coef + from_two(part[:, KV_WIDTH:])
    out_ref[:, : KV_WIDTH // 2] = total[:, : KV_WIDTH // 2].astype(out_ref.dtype)
    for head in range(KV_HEADS):
        cols = column(KV_HEADS + head)
        value = total[:, cols]
        for j in range(head * GROUP_HEADS, (head + 1) * GROUP_HEADS):
            value = value + coef[:, j : j + 1] * dir_ref[j : j + 1, :]
        out_ref[:, cols] = value.astype(out_ref.dtype)
    store_loss(out_ref, l0_ref[...] + l1_ref[...])


def group_sum(own, parts, direction, losses):
    call = in_vmem(sum_kernel, "group_sum", 7, [WIRE], meta=False)
    return call(own, *parts, direction, *losses)[0]


def sort_kernel(meta_ref, s0, s1, s2, s3, keep_ref, send_ref, loss_ref):
    total = jnp.zeros((PATCHES, KV_WIDTH), jnp.float32)
    kept = jnp.zeros((PATCHES, KV_WIDTH), jnp.float32)
    for k, part in enumerate((s0, s1, s2, s3)):
        dest = meta_ref[AT_DEST + k]
        value = part[:, :KV_WIDTH].astype(jnp.float32)
        kept = kept + jnp.where(dest == 1, value, 0.0)
        total = total + jnp.where(dest == 2, value, 0.0)
    keep_ref[...] = kept
    send_ref[:, :KV_WIDTH] = total.astype(send_ref.dtype)
    loss = (read_loss(s0) + read_loss(s2)) + (read_loss(s1) + read_loss(s3))
    store_loss(send_ref, loss)
    loss_ref[...] = loss


def sort_by_owner(meta, parts):
    grad = jax.ShapeDtypeStruct((PATCHES, KV_WIDTH), jnp.float32)
    return in_vmem(sort_kernel, "sort_by_owner", 4, [grad, WIRE, TILE])(meta, *parts)


def last_kernel(keep_ref, recv_ref, loss_in_ref, out_ref, loss_ref):
    out_ref[0] = keep_ref[...] + recv_ref[:, :KV_WIDTH].astype(jnp.float32)
    loss_ref[...] = (loss_in_ref[...] + read_loss(recv_ref))[:1, :1]


def last_sum(kept, recv, loss):
    grad = jax.ShapeDtypeStruct((1, PATCHES, KV_WIDTH), jnp.float32)
    one = jax.ShapeDtypeStruct((1, 1), jnp.float32)
    return in_vmem(last_kernel, "last_sum", 3, [grad, one], meta=False)(kept, recv, loss)


def along_y(value, step):
    pairs = [(s, s // 4 * 4 + (s + step) % 4) for s in range(8)]
    return lax.ppermute(value, "segment", pairs)


def across(value, axis, mask):
    size = lax.axis_size(axis)
    return lax.ppermute(value, axis, [(i, i ^ mask) for i in range(size)])


def per_device(
    queries, caption_kv, caption_len, image_kv, patch_count, image_list, pref_order, reward_dir
):
    idx = jnp.stack([lax.axis_index("segment"), lax.axis_index("tp")]).astype(jnp.int32)
    image = image_kv[0]
    q = queries[0]
    direction = reward_dir.reshape(KV_HEADS * GROUP_HEADS, HEAD_DIM)
    meta = make_meta(idx, image_list, patch_count, pref_order, caption_len)

    seen = [image] + [along_y(image, step) for step in (1, 2, 3)]
    wanted = pick(meta[AT_FOR_PARTNER], seen)
    own = pick(meta[AT_OWN], [*seen, across(wanted, "segment", 4)])
    acc, top, total = attend_own(q, caption_kv[0])
    others = [across(own, "tp", mask) for mask in (2, 4, 6)]
    *others, top = lax.optimization_barrier((*others, top))
    same_core = [own, *others]
    images = same_core + [across(one, "tp", 1) for one in same_core]

    keep, send, reward = attend_images(meta, q, direction, (acc, top, total), images)
    recv = across(send, "tp", 1)
    other = across(reward, "tp", 1)
    second = lax.axis_index("tp") % 2 == 1
    row = lax.broadcasted_iota(jnp.int32, reward.shape, 0)
    pair = jnp.where((row == 1) == second, reward, other)
    rewards = [pair] + [across(pair, "tp", mask) for mask in (2, 4, 6)]
    mine, to_z1, to_z2, to_z3, loss = scaled_sum(meta, keep, recv, rewards)
    parts = [across(to_z1, "tp", 2), across(to_z2, "tp", 4), across(to_z3, "tp", 6)]
    loss = loss + across(loss, "tp", 16)
    losses = (loss, across(loss, "tp", 8))
    total = group_sum(mine, parts, direction, losses)
    totals = [total] + [along_y(total, step) for step in (1, 2, 3)]
    kept, away, loss = sort_by_owner(meta, totals)
    image_grad, loss = last_sum(kept, across(away, "segment", 4), loss)
    return (loss.reshape(()), reward[0, :1], image_grad)


def solution(mesh):
    placed = (
        P(("segment", "tp"), None, None),
        P(("segment", "tp"), None, None),
        P(("segment", "tp")),
        P(("segment", "tp"), None, None),
        P(),
        P(),
        P(),
        P(),
    )
    return jax.shard_map(
        per_device,
        mesh=mesh,
        in_specs=placed,
        out_specs=(P(), P(("segment", "tp")), P(("segment", "tp"), None, None)),
        check_vma=False,
    )
```
